128 devices in a mesh: ctx: 8 (over x, z_lo), fsdp: 16 (over y, z_hi, core).
Axes of the slice: x: 4, y: 4, z: 4 (z_hi: 2, z_lo: 2; z = z_hi * 2 + z_lo), core: 2. Of those that a mesh axis runs over, the one named last changes fastest.
Arguments:
- hidden: bfloat16 [16, 2048, 8192], P('fsdp', 'ctx'), may hold values from -6 to 6
- queries: bfloat16 [16, 2048, 4096], P('fsdp', 'ctx'), may hold values from -300 to 300
- conv_input: bfloat16 [16, 2048, 8192], P('fsdp', 'ctx'), may hold values from -6 to 6
- norm_gain: float32 [8192], replicated, may hold values from 0.1 to 1.9
- kv_weight: bfloat16 [8192, 1024], P('fsdp'), may hold values from -0.0625 to 0.0625
- conv_weight: float32 [4, 8192], replicated, may hold values from -3 to 3
- conv_bias: float32 [8192], replicated, may hold values from -3 to 3
- starts: int32 [16, 8], P('fsdp'), may hold values from 0 to 2047, as said below
- segment_ids: int32 [16, 2048], P('fsdp', 'ctx'), may hold values from 0 to 7, as said below
Outputs:
- attended: bfloat16 [16, 2048, 4096], P('fsdp', 'ctx')
- conv_out: bfloat16 [16, 2048, 8192], P('fsdp', 'ctx')
The draws below stay inside these ranges and needn't reach their ends.
Inputs may be any that keep to these rules, and one draw needn't show every extreme that they name: Each row lists its 8 episode starts in increasing order, the first one 0 and the last one 2048 - 1; one episode of each row holds at least 1024 positions. `segment_ids`: in each row the ids start at 0 and rise by one at each of the row's starts.
All inputs are finite; a program needn't handle non-finite values.
Results may differ from the reference program's by a relative error of at most 0.011.
Values may be sent and summed in bfloat16 or wider, within the bound.
No kernel may reach another device: no remote copies, remote signals or barrier semaphores. Data moves between devices by JAX's collectives and lax.ppermute only.
A program may use at most 128 MiB of HBM per device.

```python
import math
import jax
import jax.numpy as jnp
from jax import lax

D = 8192
HEADS = 32
KV_HEADS = 4
HEAD = 128
CHAN = 8192
TAPS = 4
EPISODES = 8
ROWS = 16
LEN = 2048


def episode_cuts(key):
    row_keys = jax.random.split(key, ROWS)

    def one_row(row_key):
        anchor_key, order_key = jax.random.split(row_key)
        anchor = jax.random.randint(anchor_key, (), 0, LEN // 2)
        ranking = jax.random.permutation(order_key, LEN).astype(jnp.int32) + 1
        places = jnp.arange(LEN, dtype=jnp.int32)
        inside = (places > anchor) & (places < anchor + LEN // 2)
        allowed = (places >= 1) & jnp.logical_not(inside)
        ranking = jnp.where(places == LEN - 1, LEN + 1, ranking)
        ranking = jnp.where(allowed, ranking, 0)
        picked_scores, picked = lax.top_k(ranking, EPISODES - 1)
        return jnp.sort(picked.astype(jnp.int32))
    return jax.vmap(one_row)(row_keys)


def draw_starts(key, part):
    cuts = episode_cuts(key)
    return jnp.concatenate([jnp.zeros((ROWS, 1), jnp.int32), cuts], axis=1)


def draw_segment_ids(key, part):
    cuts = episode_cuts(key)
    places = jnp.arange(LEN, dtype=jnp.int32)
    return jnp.sum((cuts[:, None, :] <= places[None, :, None]).astype(jnp.int32), axis=2).astype(jnp.int32)


def draw_queries(key, part):
    key = jax.random.fold_in(key, 5)
    base_key = jax.random.fold_in(key, 0)
    values = 2.0 * jax.random.normal(base_key, (ROWS, LEN, HEADS * HEAD), jnp.float32)
    values = jnp.clip(values, -300.0, 300.0)
    return values.astype(jnp.bfloat16)


def shard_levels(stream_key, extent, cuts, low, largest):
    factor_of, own = 1.0, jax.random.fold_in(stream_key, 6)
    for dim, blocks in cuts:
        draws = jnp.exp(jax.random.uniform(jax.random.fold_in(own, dim), (blocks,), jnp.float32, low / len(cuts), largest / len(cuts)))
        factor_of = factor_of * jnp.repeat(draws, extent[dim] // blocks).reshape([-1 if axis == dim else 1 for axis in range(len(extent))])
    return factor_of


def normal_values(rng, dims, scale, limit, pieces=(), kind=jnp.bfloat16):
    values = jax.random.normal(rng, dims, jnp.float32) * scale
    if len(pieces) > 0:
        values = shard_levels(rng, dims, pieces, -0.22, 0.18) * values
    return jnp.clip(values, min=-limit, max=limit).astype(kind)


def setup_inputs(seed: int = 0) -> dict:
    seeds = jax.random.split(jax.random.key(seed), 10)
    return {
        "hidden": normal_values(seeds[0], (ROWS, LEN, D), 1.0, 6.0, ((0, 16), (1, 8))),
        "queries": draw_queries(jax.random.fold_in(seeds[9], 71), 0),
        "conv_input": normal_values(seeds[2], (ROWS, LEN, CHAN), 1.0, 6.0, ((0, 16), (1, 8))),
        "norm_gain": jnp.clip(1.0 + 0.18 * jax.random.normal(seeds[3], (D,), jnp.float32), 0.1, 1.9),
        "kv_weight": normal_values(seeds[4], (D, 2 * KV_HEADS * HEAD), D ** -0.5, 0.0625, ((0, 16),)),
        "conv_weight": normal_values(seeds[5], (TAPS, CHAN), 0.5, 3.0, (), jnp.float32),
        "conv_bias": normal_values(seeds[6], (CHAN,), 0.5, 3.0, (), jnp.float32),
        "starts": draw_starts(jax.random.fold_in(seeds[9], 71), 0),
        "segment_ids": draw_segment_ids(jax.random.fold_in(seeds[9], 71), 0),
    }


def reference(hidden, queries, conv_input, norm_gain, kv_weight, conv_weight, conv_bias, starts, segment_ids):
    kv_heads = kv_weight.shape[1] // (2 * HEAD)
    per_group = HEADS // kv_heads
    block_rows = math.gcd(LEN, 256)
    positions = jnp.arange(LEN, dtype=jnp.int32)

    def one_row(items):
        row_hidden, row_queries, row_input, row_starts, row_segments = items
        features = row_hidden.astype(jnp.float32)
        normed = (features * lax.rsqrt(lax.optimization_barrier(jnp.mean(features * features, axis=-1, keepdims=True)) + 1e-06) * norm_gain).astype(jnp.bfloat16)
        key_value = jnp.dot(normed, kv_weight, preferred_element_type=jnp.float32).astype(jnp.bfloat16)
        key_value = lax.optimization_barrier(key_value).astype(jnp.float32)
        keys = key_value[:, :kv_heads * HEAD].reshape(LEN, kv_heads, HEAD)
        values = key_value[:, kv_heads * HEAD:].reshape(LEN, kv_heads, HEAD)

        def one_block(index):
            first = (index * block_rows).astype(jnp.int32)
            query_block = lax.dynamic_slice_in_dim(row_queries, first, block_rows, 0)
            query_block = query_block.reshape(block_rows, kv_heads, per_group, HEAD).astype(jnp.float32)
            query_pos = first + jnp.arange(block_rows, dtype=jnp.int32)
            query_seg = lax.dynamic_slice_in_dim(row_segments, first, block_rows, 0)
            scores = jnp.einsum('tkgd,skd->tkgs', query_block, keys) / math.sqrt(HEAD)
            allowed = (positions[None, :] <= query_pos[:, None]) & (row_segments[None, :] == query_seg[:, None])
            allowed = allowed[:, None, None, :]
            scores = jnp.where(allowed, scores, -1e+30)
            top = lax.optimization_barrier(jnp.max(scores, axis=-1, keepdims=True))
            weights = jnp.where(allowed, jnp.exp(scores - top), 0.0)
            total = lax.optimization_barrier(jnp.sum(weights, axis=-1))
            rounded = lax.optimization_barrier(weights.astype(jnp.bfloat16)).astype(jnp.float32)
            summed = jnp.einsum('tkgs,skd->tkgd', rounded, values)
            return (summed / total[..., None]).astype(jnp.bfloat16).reshape(block_rows, HEADS * HEAD)
        attended = lax.map(one_block, jnp.arange(LEN // block_rows, dtype=jnp.int32)).reshape(LEN, HEADS * HEAD)
        episode_start = lax.optimization_barrier(jnp.max(jnp.where(row_starts[None, :] <= positions[:, None], row_starts[None, :], 0), axis=1))
        signal = row_input.astype(jnp.float32)
        padded = jnp.concatenate([jnp.zeros((TAPS - 1, CHAN), jnp.float32), signal], axis=0)
        mixing = jnp.zeros((LEN, CHAN), jnp.float32) + conv_bias[None, :]
        for tap in range(TAPS):
            source = positions - (TAPS - 1) + tap
            valid = (source >= episode_start)[:, None]
            mixing = mixing + jnp.where(valid, padded[tap:tap + LEN], 0.0) * conv_weight[tap][None, :]
        conv_out = jax.nn.silu(mixing).astype(jnp.bfloat16)
        return (attended, conv_out)
    attended, conv_out = lax.map(one_row, (hidden, queries, conv_input, starts, segment_ids))
    return (attended, conv_out)
```

```python
import functools
import math

import jax
import jax.numpy as jnp
import numpy as np
from jax import lax
from jax.experimental import pallas as pl
from jax.experimental.pallas import tpu as pltpu
from jax.sharding import PartitionSpec as P

HEAD = 128
TAPS = 4
EPISODES = 8
AXES = ("ctx", "fsdp")
CTX, FSDP = 8, 16
DEVICES = CTX * FSDP
MIB = 1 << 20


def place(i):
    c, f = divmod(i, FSDP)
    x, zl = divmod(c, 2)
    y, r = divmod(f, 4)
    zh, k = divmod(r, 2)
    return x, y, zh, zl, k


def device(x, y, zh, zl, k):
    return ((x % 4) * 2 + zl) * FSDP + ((y % 4) * 2 + zh) * 2 + k


def lead_core(x, zl):
    return (x + zl) % 2


def neighbour(x, y, zh, zl, way):
    return {
        "x+": (x + 1, y, zh, zl),
        "x-": (x - 1, y, zh, zl),
        "y+": (x, y + 1, zh, zl),
        "y-": (x, y - 1, zh, zl),
        "zlo": (x, y, zh, 1 - zl),
        "zhi": (x, y, 1 - zh, 1 - zl),
    }[way]


STEPS = (
    ((0, "y-", 0), (1, "zhi", 1)),
    ((0, "y+", 1),),
    ((0, "x-", 1), (1, "x+", 0)),
    ((0, "y-", 0), (1, "y+", 1)),
    ((0, "zhi", 0), (1, "zlo", 1)),
    ((0, "x-", 0), (1, "x+", 1)),
    ((0, "zlo", 1), (1, "y+", 0)),
    ((0, "y-", 0),),
)
SENT = ((0, 0), (0, 0), (1, 2), (1, 1), (1, 1), (4, 4), (5, 4), (5, 5))


def weight_plan():
    pairs, held = [], [[i % FSDP for i in range(DEVICES)]]
    for step, sent in zip(STEPS, SENT):
        now, got = [], [-1] * DEVICES
        for i in range(DEVICES):
            x, y, zh, zl, k = place(i)
            role = 0 if k == lead_core(x, zl) else 1
            for sender, way, receiver in step:
                if sender == role:
                    nx, ny, nzh, nzl = neighbour(x, y, zh, zl, way)
                    lead = lead_core(nx, nzl)
                    to = device(nx, ny, nzh, nzl, lead if receiver == 0 else 1 - lead)
                    now.append((i, to))
                    got[to] = held[sent[role]][i]
        pairs.append(now)
        held.append(got)
    slots = [
        [held[n][i] for n in (0, 1, 3, 4, 5, 6, 7)] + [max(held[2][i], held[8][i])]
        for i in range(DEVICES)
    ]
    return pairs, np.asarray(slots, np.int32)


WEIGHT_PAIRS, SLOTS = weight_plan()


def moved(way):
    return [
        (i, device(*neighbour(*place(i)[:4], way), place(i)[4])) for i in range(DEVICES)
    ]


SWAP = [(i, i ^ 1) for i in range(DEVICES)]


def send(x, pairs):
    return lax.ppermute(x, AXES, pairs)


def params(mib, **kw):
    return pltpu.CompilerParams(vmem_limit_bytes=mib * MIB, **kw)


def cost(flops, moved_bytes, trans=0):
    return pl.CostEstimate(
        flops=int(flops), bytes_accessed=int(moved_bytes), transcendentals=int(trans)
    )


def norm_kernel(slots, h_ref, g_ref, mine_ref, other_ref, *, width, chunk, count):
    rows = h_ref.shape[0]
    total = jnp.zeros((rows, chunk), jnp.float32)
    for c in range(width // chunk):
        f = h_ref[:, c * chunk : (c + 1) * chunk].astype(jnp.float32)
        total = total + f * f
    mean = jnp.sum(total, axis=-1, keepdims=True) * (1.0 / width)
    factor = lax.rsqrt(mean + 1e-06)
    for which, out in ((1, other_ref), (0, mine_ref)):
        for s in range(count):
            at = pl.multiple_of(slots[which, s] * chunk, chunk)
            f = h_ref[:, pl.ds(at, chunk)].astype(jnp.float32)
            out[s] = (f * factor * g_ref[:, pl.ds(at, chunk)]).astype(jnp.bfloat16)


def norm(slots, hidden, gain, chunk):
    rows, width = hidden.shape
    count = slots.shape[1]
    tile = 64
    shape = jax.ShapeDtypeStruct((count, rows, chunk), jnp.bfloat16)
    out_spec = pl.BlockSpec((count, tile, chunk), lambda i: (0, i, 0))
    return pl.pallas_call(
        functools.partial(norm_kernel, width=width, chunk=chunk, count=count),
        grid=(rows // tile,),
        in_specs=[
            pl.BlockSpec(memory_space=pltpu.SMEM),
            pl.BlockSpec((tile, width), lambda i: (i, 0)),
            pl.BlockSpec((1, width), lambda i: (0, 0)),
        ],
        out_specs=[out_spec, out_spec],
        out_shape=[shape, shape],
        compiler_params=params(24),
        cost_estimate=cost(rows * width * 6, rows * width * 4),
        name="norm",
    )(slots, hidden, gain)


def project_kernel(*refs, count, carried):
    xs, ws = refs[:count], refs[count : 2 * count]
    out = refs[-1]
    total = refs[2 * count][...] if carried else None
    for x, w in zip(xs, ws):
        part = jnp.dot(x[0], w[...], preferred_element_type=jnp.float32)
        total = part if total is None else total + part
    out[...] = total


def project(x, slots, weights, carried=None):
    _, rows, depth = x.shape
    columns = weights[0].shape[1]
    tile = 512
    count = len(slots)
    in_specs = [
        pl.BlockSpec((1, rows, depth), functools.partial(lambda s, i: (s, 0, 0), s)) for s in slots
    ]
    in_specs += [pl.BlockSpec((depth, tile), lambda i: (0, i))] * count
    out_spec = pl.BlockSpec((rows, tile), lambda i: (0, i))
    operands = [x] * count + list(weights)
    if carried is not None:
        in_specs.append(out_spec)
        operands.append(carried)
    return pl.pallas_call(
        functools.partial(project_kernel, count=count, carried=carried is not None),
        grid=(columns // tile,),
        in_specs=in_specs,
        out_specs=out_spec,
        out_shape=jax.ShapeDtypeStruct((rows, columns), jnp.float32),
        compiler_params=params(24),
        cost_estimate=cost(
            2 * count * rows * depth * columns, count * (rows + columns) * depth * 2 + rows * columns * 8
        ),
        name="project",
    )(*operands)


def conv_kernel(info, x_ref, halo_ref, w_ref, b_ref, o_ref, ext):
    rows, width = x_ref.shape
    back = TAPS - 1
    ext[pl.ds(8 - back, back), :] = halo_ref[...].astype(jnp.float32)
    ext[pl.ds(8, rows), :] = x_ref[...].astype(jnp.float32)
    step, lanes = 32, 256
    for r in range(0, rows, step):
        pos = info[0] + r + lax.broadcasted_iota(jnp.int32, (step, 1), 0)
        begin = jnp.zeros((step, 1), jnp.int32)
        for e in range(EPISODES):
            begin = jnp.where(info[1 + e] <= pos, jnp.maximum(begin, info[1 + e]), begin)
        depth = pos - begin
        for c in range(0, width, lanes):
            cols = slice(c, c + lanes)
            mixing = jnp.zeros((step, lanes), jnp.float32) + b_ref[:, cols]
            for tap in range(TAPS):
                behind = back - tap
                term = ext[pl.ds(8 + r - behind, step), cols]
                if behind:
                    term = jnp.where(depth >= behind, term, 0.0)
                mixing = mixing + term * w_ref[tap : tap + 1, cols]
            o_ref[pl.ds(r, step), cols] = (mixing / (1.0 + jnp.exp(-mixing))).astype(o_ref.dtype)


def conv(info, x, halo, weight, bias):
    rows, width = x.shape
    tile = 1024
    return pl.pallas_call(
        conv_kernel,
        grid=(width // tile,),
        in_specs=[
            pl.BlockSpec(memory_space=pltpu.SMEM),
            pl.BlockSpec((rows, tile), lambda i: (0, i)),
            pl.BlockSpec((TAPS - 1, tile), lambda i: (0, i)),
            pl.BlockSpec((TAPS, tile), lambda i: (0, i)),
            pl.BlockSpec((1, tile), lambda i: (0, i)),
        ],
        out_specs=pl.BlockSpec((rows, tile), lambda i: (0, i)),
        out_shape=jax.ShapeDtypeStruct((rows, width), x.dtype),
        scratch_shapes=[pltpu.VMEM((rows + 8, tile), jnp.float32)],
        compiler_params=params(24),
        cost_estimate=cost(rows * width * 40, rows * width * 4, rows * width * 2),
        name="conv",
    )(info, x, halo, weight, bias)


def attend_kernel(info, q_ref, *refs, count, per_group):
    ks, vs = refs[:count], refs[count : 2 * count]
    o_ref, m_ref, l_ref, a_ref, mask_ref = refs[2 * count :]
    rows = q_ref.shape[0]
    keys = ks[0].shape[0]
    factor = math.log2(math.e) / math.sqrt(HEAD)
    first = info[0]
    pos = first + lax.broadcasted_iota(jnp.int32, (rows, keys), 0)
    begin = jnp.zeros((rows, keys), jnp.int32)
    lowest = jnp.int32(0)
    for e in range(EPISODES):
        start = info[1 + e]
        begin = jnp.where(start <= pos, jnp.maximum(begin, start), begin)
        lowest = jnp.where(start <= first, jnp.maximum(lowest, start), lowest)
    offset = lax.broadcasted_iota(jnp.int32, (rows, keys), 1)

    def block(b, own):
        key_pos = info[1 + EPISODES + b] + offset
        allowed = key_pos >= begin
        if own:
            allowed = allowed & (key_pos <= pos)
        mask_ref[...] = jnp.where(allowed, 0.0, -1e30)
        for h in range(per_group):
            q = q_ref[:, h * HEAD : (h + 1) * HEAD]
            s = lax.dot_general(
                q, ks[b][...], (((1,), (1,)), ((), ())), preferred_element_type=jnp.float32
            )
            s = s + mask_ref[...]
            top = jnp.max(s, axis=1, keepdims=True)
            if own:
                new = jnp.broadcast_to(top, (rows, HEAD))
            else:
                old = m_ref[h]
                new = jnp.maximum(old, top)
            w = jnp.exp2((s - jnp.concatenate([new] * (keys // HEAD), axis=1)) * factor)
            part = w[:, :HEAD]
            for c in range(HEAD, keys, HEAD):
                part = part + w[:, c : c + HEAD]
            product = jnp.dot(
                w.astype(jnp.bfloat16), vs[b][...], preferred_element_type=jnp.float32
            )
            if own:
                l_ref[h] = part
                a_ref[h] = product
            else:
                shrink = jnp.exp2((old - new) * factor)
                l_ref[h] = l_ref[h] * shrink + part
                a_ref[h] = a_ref[h] * shrink + product
            m_ref[h] = new

    block(0, True)
    for b in range(1, count):
        base = info[1 + EPISODES + b]

        @pl.when((base < first) & (base + keys > lowest))
        def _():
            block(b, False)

    for h in range(per_group):
        total = jnp.sum(l_ref[h], axis=1, keepdims=True)
        o_ref[:, h * HEAD : (h + 1) * HEAD] = (a_ref[h] / total).astype(o_ref.dtype)


def attend(info, queries, blocks):
    rows, width = queries.shape
    keys, columns = blocks[0].shape
    kv_heads = columns // (2 * HEAD)
    group = width // kv_heads
    count = len(blocks)
    per_group = group // HEAD
    q_spec = pl.BlockSpec((rows, group), lambda g: (0, g))
    return pl.pallas_call(
        functools.partial(attend_kernel, count=count, per_group=per_group),
        grid=(kv_heads,),
        in_specs=[pl.BlockSpec(memory_space=pltpu.SMEM), q_spec]
        + [pl.BlockSpec((keys, HEAD), lambda g: (0, g))] * count
        + [pl.BlockSpec((keys, HEAD), lambda g: (0, kv_heads + g))] * count,
        out_specs=q_spec,
        out_shape=jax.ShapeDtypeStruct((rows, width), queries.dtype),
        scratch_shapes=[pltpu.VMEM((per_group, rows, HEAD), jnp.float32)] * 3
        + [pltpu.VMEM((rows, keys), jnp.float32)],
        compiler_params=params(32),
        cost_estimate=cost(
            4 * rows * width * keys * count, rows * width * 4 + count * keys * columns * 2,
            rows * keys * count * width // HEAD,
        ),
        name="attend",
    )(info, queries, *blocks, *blocks)


def body(
    hidden, queries, conv_input, norm_gain, kv_weight, conv_weight, conv_bias, starts, segment_ids
):
    del segment_ids
    rows = hidden.shape[1]
    ctx = lax.axis_index("ctx")
    me = ctx * FSDP + lax.axis_index("fsdp")
    x, zl = ctx // 2, ctx % 2
    leads = lax.axis_index("fsdp") % 2 == lead_core(x, zl)
    depth = kv_weight.shape[0]

    w1 = send(kv_weight, WEIGHT_PAIRS[0])
    w2 = send(kv_weight, WEIGHT_PAIRS[1])

    table = jnp.asarray(SLOTS)
    slots = jnp.stack([table[me], table[me ^ 1]])
    mine, other = norm(slots, hidden[0], norm_gain[None], depth)
    theirs = send(other, SWAP)

    w3 = send(jnp.where(leads, w1, w2), WEIGHT_PAIRS[2])
    w4 = send(w1, WEIGHT_PAIRS[3])
    w5 = send(w1, WEIGHT_PAIRS[4])

    first = ctx * rows
    info = jnp.concatenate([first[None], starts[0]])
    signal = conv_input[0]
    halo = lax.ppermute(
        signal[rows - (TAPS - 1) :], "ctx", [(i, i + 1) for i in range(CTX - 1)]
    )
    conv_out = conv(info, signal, halo, conv_weight, conv_bias[None])

    def both(slot_ids, weights, carried=(None, None)):
        return tuple(
            project(v, slot_ids, weights, c) for v, c in zip((theirs, mine), carried)
        )

    sums = both((0, 1), (kv_weight, w1))
    w6 = send(w4, WEIGHT_PAIRS[5])
    w7 = send(jnp.where(leads, w5, w4), WEIGHT_PAIRS[6])
    w8 = send(w5, WEIGHT_PAIRS[7])
    sums = both((2, 3, 4), (w3, w4, w5), sums)
    last = (w6, w7, jnp.where(leads, w8, w2))
    their_sum = project(theirs, (5, 6, 7), last, sums[0])
    back = send(their_sum, SWAP)
    my_sum = project(mine, (5, 6, 7), last, sums[1])
    kv = (my_sum + back).astype(jnp.bfloat16)

    up, down, pair = moved("x+"), moved("x-"), moved("zlo")
    from_left = send(kv, up)
    from_right = send(kv, down)
    from_pair = send(kv, pair)
    left_pair = send(from_pair, up)
    right_pair = send(from_pair, down)
    far = send(from_left, up)
    far_pair = send(right_pair, down)

    def base(dx, dz):
        return (((x + dx) % 4) * 2 + (zl + dz) % 2) * rows

    bases = [first, base(0, 1), base(-1, 0), base(1, 0), base(-1, 1), base(1, 1), base(2, 0), base(2, 1)]
    blocks = [kv, from_pair, from_left, from_right, left_pair, right_pair, far, far_pair]
    attended = attend(jnp.concatenate([info, jnp.stack(bases)]), queries[0], blocks)
    return attended[None], conv_out[None]


def solution(mesh):
    return jax.shard_map(
        body,
        mesh=mesh,
        in_specs=(
            P("fsdp", "ctx", None),
            P("fsdp", "ctx", None),
            P("fsdp", "ctx", None),
            P(),
            P("fsdp", None),
            P(),
            P(),
            P("fsdp", None),
            P("fsdp", "ctx"),
        ),
        out_specs=(P("fsdp", "ctx", None), P("fsdp", "ctx", None)),
        check_vma=False,
    )
```

```python
import functools
import math

import jax
import jax.numpy as jnp
import numpy as np
from jax import lax
from jax.experimental import pallas as pl
from jax.experimental.pallas import tpu as pltpu
from jax.sharding import PartitionSpec as P

HEAD = 128
TAPS = 4
EPISODES = 8
AXES = ("ctx", "fsdp")
CTX, FSDP = 8, 16
DEVICES = CTX * FSDP
MIB = 1 << 20


def place(i):
    c, f = divmod(i, FSDP)
    x, zl = divmod(c, 2)
    y, r = divmod(f, 4)
    zh, k = divmod(r, 2)
    return x, y, zh, zl, k


def device(x, y, zh, zl, k):
    return ((x % 4) * 2 + zl) * FSDP + ((y % 4) * 2 + zh) * 2 + k


def lead_core(x, zl):
    return (x + zl) % 2


def neighbour(x, y, zh, zl, way):
    return {
        "x+": (x + 1, y, zh, zl),
        "x-": (x - 1, y, zh, zl),
        "y+": (x, y + 1, zh, zl),
        "y-": (x, y - 1, zh, zl),
        "zlo": (x, y, zh, 1 - zl),
        "zhi": (x, y, 1 - zh, 1 - zl),
    }[way]


STEPS = (
    ((0, "y-", 0), (1, "zhi", 1)),
    ((0, "y+", 1),),
    ((0, "x-", 1), (1, "zlo", 0)),
    ((0, "y-", 0), (1, "y+", 1)),
    ((0, "zhi", 0), (1, "x+", 1)),
    ((0, "x-", 0), (1, "x+", 1)),
    ((0, "y-", 1), (1, "y+", 0)),
    ((0, "zlo", 0),),
)
SENT = ((0, 0), (0, 0), (1, 1), (1, 1), (1, 2), (4, 4), (5, 4), (5, 5))
SLOT_STEPS = ((0, 0), (1, 1), (3, 3), (4, 4), (5, 5), (6, 6), (7, 7), (8, 2))


def role_of(i):
    x, _, _, zl, k = place(i)
    return 0 if k == lead_core(x, zl) else 1


def weight_plan():
    pairs, held = [], [[i % FSDP for i in range(DEVICES)]]
    for step, sent in zip(STEPS, SENT):
        now, got = [], [-1] * DEVICES
        for i in range(DEVICES):
            for sender, way, receiver in step:
                if sender == role_of(i):
                    nx, ny, nzh, nzl = neighbour(*place(i)[:4], way)
                    lead = lead_core(nx, nzl)
                    to = device(nx, ny, nzh, nzl, lead if receiver == 0 else 1 - lead)
                    now.append((i, to))
                    got[to] = held[sent[role_of(i)]][i]
        pairs.append(now)
        held.append(got)
    slots = [[held[step[role_of(i)]][i] for step in SLOT_STEPS] for i in range(DEVICES)]
    return pairs, np.asarray(slots, np.int32)


WEIGHT_PAIRS, SLOTS = weight_plan()


def moved(way, wanted):
    pairs = [(i, device(*neighbour(*place(i)[:4], way), place(i)[4])) for i in range(DEVICES)]
    return [(i, to) for i, to in pairs if wanted(place(to)[0], place(to)[3])]


SWAP = [(i, i ^ 1) for i in range(DEVICES)]


def send(x, pairs):
    return lax.ppermute(x, AXES, pairs)


def together(*values):
    return lax.optimization_barrier(values)


def params(mib, **kw):
    return pltpu.CompilerParams(vmem_limit_bytes=mib * MIB, **kw)


WHOLE = pl.BlockSpec(memory_space=pltpu.VMEM)
SCALARS = pl.BlockSpec(memory_space=pltpu.SMEM)
BLOCKS = 8
LEAD = 1 + EPISODES + BLOCKS


def hand_on(scalars, token):
    for i in range(LEAD + 1):
        token[i] = scalars[i]


def cost(flops, moved_bytes, trans=0):
    return pl.CostEstimate(
        flops=int(flops), bytes_accessed=int(moved_bytes), transcendentals=int(trans)
    )


def norm_kernel(slots, h_ref, g_ref, mine_ref, other_ref, *, width, chunk, count):
    rows = h_ref.shape[0]
    here = pl.ds(pl.multiple_of(pl.program_id(0) * rows, rows), rows)
    total = jnp.zeros((rows, chunk), jnp.float32)
    for c in range(width // chunk):
        f = h_ref[:, c * chunk : (c + 1) * chunk].astype(jnp.float32)
        total = total + f * f
    mean = jnp.sum(total, axis=-1, keepdims=True) * (1.0 / width)
    factor = lax.rsqrt(mean + 1e-06)
    for which, out in ((1, other_ref), (0, mine_ref)):
        for s in range(count):
            at = pl.multiple_of(slots[which, s] * chunk, chunk)
            f = h_ref[:, pl.ds(at, chunk)].astype(jnp.float32)
            out[s, here, :] = (f * factor * g_ref[:, pl.ds(at, chunk)]).astype(jnp.bfloat16)


def norm(slots, hidden, gain, chunk):
    rows, width = hidden.shape
    count = slots.shape[1]
    tile = 64
    shape = pltpu.VMEM((count, rows, chunk), jnp.bfloat16)
    return pl.pallas_call(
        functools.partial(norm_kernel, width=width, chunk=chunk, count=count),
        grid=(rows // tile,),
        in_specs=[
            pl.BlockSpec(memory_space=pltpu.SMEM),
            pl.BlockSpec((tile, width), lambda i: (i, 0)),
            pl.BlockSpec((1, width), lambda i: (0, 0)),
        ],
        out_specs=[WHOLE, WHOLE],
        out_shape=[shape, shape],
        compiler_params=params(16),
        cost_estimate=cost(rows * width * 6, rows * width * 2),
        name="norm",
    )(slots, hidden, gain)


def project_kernel(scalars, *refs, sides, slots, counts, carried):
    xs, ws = refs[:sides], refs[sides : sides + sum(counts)]
    olds = refs[sides + sum(counts) :][:carried]
    outs, token = refs[-1 - sides : -1], refs[-1]
    hand_on(scalars, token)
    tile = 256
    at = 0
    for s, n in enumerate(counts):
        for c in range(0, ws[at].shape[1], tile):
            cols = slice(c, c + tile)
            w = ws[at][:, cols]
            if n == 2:
                w = jnp.where(scalars[LEAD] > 0, w, ws[at + 1][:, cols])
            for side in range(sides):
                part = jnp.dot(xs[side][slots[s]], w, preferred_element_type=jnp.float32)
                if s:
                    part = outs[side][:, cols] + part
                elif carried:
                    part = olds[side][:, cols] + part
                outs[side][:, cols] = part
        at += n


def project(scalars, xs, slots, weights, carried=()):
    _, rows, depth = xs[0].shape
    weights = [w if isinstance(w, tuple) else (w,) for w in weights]
    counts = tuple(len(w) for w in weights)
    flat = [v for w in weights for v in w]
    columns = flat[0].shape[1]
    sides, count = len(xs), len(slots)
    inside = [pltpu.with_memory_space_constraint(v, pltpu.VMEM) for v in (*xs, *flat, *carried)]
    return pl.pallas_call(
        functools.partial(
            project_kernel, sides=sides, slots=slots, counts=counts, carried=len(carried)
        ),
        in_specs=[SCALARS] + [WHOLE] * len(inside),
        out_specs=[WHOLE] * sides + [SCALARS],
        out_shape=[pltpu.VMEM((rows, columns), jnp.float32)] * sides
        + [jax.ShapeDtypeStruct(scalars.shape, scalars.dtype)],
        compiler_params=params(8),
        cost_estimate=cost(2 * sides * count * rows * depth * columns, rows * columns * 4),
        name="project",
    )(scalars, *inside)


def pick_kernel(scalars, a_ref, b_ref, o_ref, token):
    hand_on(scalars, token)

    @pl.when(scalars[LEAD] > 0)
    def _():
        o_ref[...] = a_ref[...]

    @pl.when(scalars[LEAD] <= 0)
    def _():
        o_ref[...] = b_ref[...]


def pick(scalars, a, b):
    inside = [pltpu.with_memory_space_constraint(v, pltpu.VMEM) for v in (a, b)]
    return pl.pallas_call(
        pick_kernel,
        in_specs=[SCALARS, WHOLE, WHOLE],
        out_specs=[WHOLE, SCALARS],
        out_shape=[
            pltpu.VMEM(a.shape, a.dtype),
            jax.ShapeDtypeStruct(scalars.shape, scalars.dtype),
        ],
        compiler_params=params(8),
        cost_estimate=cost(a.size, a.size),
        name="pick",
    )(scalars, *inside)


def add_kernel(a_ref, b_ref, o_ref):
    o_ref[...] = (a_ref[...] + b_ref[...]).astype(o_ref.dtype)


def add(a, b):
    inside = [pltpu.with_memory_space_constraint(v, pltpu.VMEM) for v in (a, b)]
    return pl.pallas_call(
        add_kernel,
        in_specs=[WHOLE, WHOLE],
        out_specs=WHOLE,
        out_shape=pltpu.VMEM(a.shape, jnp.bfloat16),
        compiler_params=params(8),
        cost_estimate=cost(a.size, a.size),
        name="add",
    )(*inside)


def conv_kernel(info, x_ref, halo_ref, w_ref, b_ref, o_ref, token, pick, before):
    rows, width = x_ref.shape
    ahead = halo_ref.shape[0]
    hand_on(info, token)

    @pl.when(pl.program_id(0) == 0)
    def _():
        before[...] = halo_ref[...]

    shape = (rows, ahead + rows)
    pos = info[0] + pl.program_id(0) * rows + lax.broadcasted_iota(jnp.int32, shape, 0)
    begin = jnp.zeros(shape, jnp.int32)
    for e in range(EPISODES):
        begin = jnp.where(info[1 + e] <= pos, jnp.maximum(begin, info[1 + e]), begin)
    apart = lax.broadcasted_iota(jnp.int32, shape, 0) + ahead - lax.broadcasted_iota(jnp.int32, shape, 1)
    for tap in range(TAPS):
        behind = TAPS - 1 - tap
        taken = (apart == behind) & (pos - behind >= begin)
        pick[tap * rows : (tap + 1) * rows, :] = jnp.where(taken, 1.0, 0.0).astype(pick.dtype)

    lanes = 256
    for c in range(0, width, lanes):
        cols = slice(c, c + lanes)
        source = jnp.concatenate([before[:, cols], x_ref[:, cols]], axis=0)
        taps = jnp.dot(pick[...], source, preferred_element_type=jnp.float32)
        mixing = b_ref[:, cols] + taps[:rows] * w_ref[0:1, cols]
        for tap in range(1, TAPS):
            mixing = mixing + taps[tap * rows : (tap + 1) * rows] * w_ref[tap : tap + 1, cols]
        by_half = 0.5 * mixing
        o_ref[:, cols] = (by_half + by_half * jnp.tanh(by_half)).astype(o_ref.dtype)
    before[...] = x_ref[rows - ahead :, :]


def conv(info, x, halo, weight, bias):
    rows, width = x.shape
    tile = 64
    ahead = halo.shape[0]
    full = lambda n: pl.BlockSpec((n, width), lambda i: (0, 0))
    return pl.pallas_call(
        conv_kernel,
        grid=(rows // tile,),
        in_specs=[
            SCALARS,
            pl.BlockSpec((tile, width), lambda i: (i, 0)),
            full(ahead),
            full(TAPS),
            full(1),
        ],
        out_specs=[pl.BlockSpec((tile, width), lambda i: (i, 0)), SCALARS],
        out_shape=[
            jax.ShapeDtypeStruct((rows, width), x.dtype),
            jax.ShapeDtypeStruct(info.shape, info.dtype),
        ],
        scratch_shapes=[
            pltpu.VMEM((TAPS * tile, ahead + tile), jnp.bfloat16),
            pltpu.VMEM((ahead, width), x.dtype),
        ],
        compiler_params=params(16),
        cost_estimate=cost(rows * width * 40, rows * width * 4, rows * width),
        name="conv",
    )(info, x, halo, weight, bias)


def attend_kernel(info, q_ref, *refs, pieces, per_group, stage, at):
    count = len(pieces)

    ks, vs = refs[: sum(pieces)], refs[sum(pieces) : 2 * sum(pieces)]
    rest = refs[2 * sum(pieces) :]
    if stage == "first":
        m_ref, a_ref, token, mask_ref = rest
        m_in, a_in = m_ref, a_ref
        hand_on(info, token)
    elif stage == "middle":
        m_in, a_in, m_ref, a_ref, token, mask_ref = rest
        hand_on(info, token)
    else:
        m_in, a_in, o_ref, mask_ref = rest
    rows = q_ref.shape[0]
    keys = mask_ref.shape[1]
    factor = math.log2(math.e) / math.sqrt(HEAD)
    first = info[0]
    lowest = jnp.int32(0)
    for e in range(EPISODES):
        start = info[1 + e]
        lowest = jnp.where(start <= first, jnp.maximum(lowest, start), lowest)
    head = pl.program_id(0) * per_group

    def loaded(parts, b):
        at = sum(pieces[:b])
        values = [r[...] for r in parts[at : at + pieces[b]]]
        return values[0] if len(values) == 1 else jnp.concatenate(values, axis=0)

    def divided(h, a):
        o_ref[:, h * HEAD : (h + 1) * HEAD] = (a[:, :HEAD] / a[:, HEAD:]).astype(o_ref.dtype)

    def block(b):
        pos = first + lax.broadcasted_iota(jnp.int32, (rows, keys), 0)
        key_pos = info[1 + EPISODES + at + b] + lax.broadcasted_iota(jnp.int32, (rows, keys), 1)
        begin = jnp.zeros((rows, keys), jnp.int32)
        for e in range(EPISODES):
            begin = jnp.where(info[1 + e] <= pos, jnp.maximum(begin, info[1 + e]), begin)
        allowed = (key_pos >= begin) & (key_pos <= pos)
        mask_ref[...] = jnp.where(allowed, 0.0, -1e30)
        k, v = loaded(ks, b), loaded(vs, b)
        v = jnp.concatenate([v, jnp.ones_like(v)], axis=1)
        for h in range(per_group):
            q = q_ref[:, h * HEAD : (h + 1) * HEAD]
            s = lax.dot_general(
                q, k, (((1,), (1,)), ((), ())), preferred_element_type=jnp.float32
            )
            s = s + mask_ref[...]
            top = jnp.max(s, axis=1, keepdims=True)
            if stage == "first":
                new = jnp.broadcast_to(top, (rows, HEAD))
            else:
                old = m_in[head + h]
                new = jnp.maximum(old, top)
            w = jnp.exp2((s - jnp.concatenate([new] * (keys // HEAD), axis=1)) * factor)
            a = jnp.dot(w.astype(jnp.bfloat16), v, preferred_element_type=jnp.float32)
            if stage != "first":
                shrink = jnp.exp2((old - new) * factor)
                a = a_in[head + h] * jnp.concatenate([shrink, shrink], axis=1) + a
            if stage == "last":
                divided(h, a)
            else:
                a_ref[head + h] = a
                m_ref[head + h] = new

    for b in range(count):
        if stage == "first":
            block(b)
            continue
        base = info[1 + EPISODES + at + b]
        live = (base < first) & (base + keys > lowest)
        pl.when(live)(functools.partial(block, b))
        if stage == "last":

            @pl.when(jnp.logical_not(live))
            def _():
                for h in range(per_group):
                    divided(h, a_in[head + h])


def attend(stage, scalars, at, queries, blocks, state=()):
    rows, width = queries.shape
    blocks = [b if isinstance(b, tuple) else (b,) for b in blocks]
    flat = [v for b in blocks for v in b]
    pieces = [len(b) for b in blocks]
    columns = flat[0].shape[1]
    kv_heads = columns // (2 * HEAD)
    group = width // kv_heads
    heads = width // HEAD
    keys = sum(v.shape[0] for v in blocks[0])
    assert stage != "last" or len(blocks) == 1
    q_spec = pl.BlockSpec((rows, group), lambda g: (0, g))
    if stage == "last":
        out_shape = jax.ShapeDtypeStruct((rows, width), queries.dtype)
        out_specs = q_spec
    else:
        out_shape = [
            pltpu.VMEM((heads, rows, HEAD), jnp.float32),
            pltpu.VMEM((heads, rows, 2 * HEAD), jnp.float32),
            jax.ShapeDtypeStruct(scalars.shape, scalars.dtype),
        ]
        out_specs = [WHOLE, WHOLE, SCALARS]
    in_specs = [pl.BlockSpec(memory_space=pltpu.SMEM), q_spec]
    in_specs += [pl.BlockSpec((v.shape[0], HEAD), lambda g: (0, g)) for v in flat]
    in_specs += [pl.BlockSpec((v.shape[0], HEAD), lambda g: (0, kv_heads + g)) for v in flat]
    in_specs += [WHOLE] * len(state)
    aliases = {} if stage != "middle" else {len(in_specs) - 2: 0, len(in_specs) - 1: 1}
    state = [pltpu.with_memory_space_constraint(v, pltpu.VMEM) for v in state]
    return pl.pallas_call(
        functools.partial(
            attend_kernel, pieces=pieces, per_group=group // HEAD, stage=stage, at=at
        ),
        grid=(kv_heads,),
        in_specs=in_specs,
        out_specs=out_specs,
        out_shape=out_shape,
        input_output_aliases=aliases,
        scratch_shapes=[pltpu.VMEM((rows, keys), jnp.float32)],
        compiler_params=params(12),
        cost_estimate=cost(
            4 * rows * width * keys * len(blocks),
            rows * width * 2 + keys * columns * 2 * len(blocks),
            rows * keys * len(blocks) * heads,
        ),
        name="attend_" + stage,
    )(scalars, queries, *flat, *flat, *state)


def body(
    hidden, queries, conv_input, norm_gain, kv_weight, conv_weight, conv_bias, starts, segment_ids
):
    del segment_ids
    rows = hidden.shape[1]
    ctx = lax.axis_index("ctx")
    me = ctx * FSDP + lax.axis_index("fsdp")
    x, zl = ctx // 2, ctx % 2
    depth = kv_weight.shape[0]
    leads = lax.axis_index("fsdp") % 2 == lead_core(x, zl)
    table = jnp.asarray(SLOTS)
    slots = jnp.stack([table[me], table[me ^ 1]])

    def base(dx, dz):
        return (((x + dx) % 4) * 2 + (zl + dz) % 2) * rows

    bases = [base(0, 0), base(0, 1), base(-1, 0), base(1, 0), base(-1, 1), base(2, 0), base(1, 1), base(2, 1)]
    scalars = jnp.concatenate(
        [(ctx * rows)[None], starts[0], jnp.stack(bases), leads.astype(jnp.int32)[None]]
    )
    signal = conv_input[0]
    tail = signal[rows - 16 :]
    scalars, slots, tail = together(scalars, slots, tail)

    w0 = kv_weight
    w1 = send(w0, WEIGHT_PAIRS[0])
    w2 = send(w0, WEIGHT_PAIRS[1])
    halo = lax.ppermute(tail, "ctx", [(i, i + 1) for i in range(CTX - 1)])
    mine, other = norm(slots, hidden[0], norm_gain[None], depth)
    w1, w2, halo, mine, other = together(w1, w2, halo, mine, other)

    w4 = send(w1, WEIGHT_PAIRS[3])
    theirs = send(other, SWAP)
    picked, scalars = pick(scalars, w1, w2)
    w5 = send(picked, WEIGHT_PAIRS[4])
    w1_later, scalars = together(w1, scalars)
    w3 = send(w1_later, WEIGHT_PAIRS[2])
    *sums, scalars = project(scalars, (theirs, mine), (0, 1), (w0, w1))

    w4, w5, scalars = together(w4, w5, scalars)
    w6 = send(w4, WEIGHT_PAIRS[5])
    picked, scalars = pick(scalars, w5, w4)
    w7 = send(picked, WEIGHT_PAIRS[6])
    w8 = send(w5, WEIGHT_PAIRS[7])
    conv_out, scalars = conv(scalars, signal, halo, conv_weight, conv_bias[None])
    *sums, scalars = project(scalars, (theirs, mine), (2, 3, 4), (w3, w4, w5), sums)

    last = ((5, 6, 7), (w6, w7, (w8, w2)))
    their_sum, _ = project(scalars, (theirs,), *last, (sums[0],))
    back = send(their_sum, SWAP)
    my_sum, _ = project(scalars, (mine,), *last, (sums[1],))
    kv = add(my_sum, back)

    half = rows // 2
    right_end = (0, 3)
    q = queries[0]
    from_right = send(kv, moved("x-", lambda x, z: x in right_end))
    from_pair = send(kv, moved("zlo", lambda x, z: x < 3 or z == 1))
    from_left = send(kv, moved("x+", lambda x, z: x > 0))
    *state, scalars = attend("first", scalars, 0, q, [kv])
    from_right, from_pair, scalars = together(from_right, from_pair, scalars)
    left_pair = send(from_pair, moved("x+", lambda x, z: x > 0))
    right_pair = send(from_right, moved("zlo", lambda x, z: x in right_end))
    far = send(from_right, moved("x-", lambda x, z: x > 1))
    *state, scalars = attend(
        "middle",
        scalars,
        1,
        q,
        [from_pair, from_left, from_right],
        state,
    )
    left_pair, right_pair, scalars = together(left_pair, right_pair, scalars)
    far_top = send(left_pair[:half], moved("x+", lambda x, z: x > 1))
    far_bottom = send(right_pair[half:], moved("x-", lambda x, z: x > 1))
    *state, scalars = attend(
        "middle",
        scalars,
        4,
        q,
        [left_pair, far, right_pair],
        state,
    )
    attended = attend("last", scalars, 7, q, [(far_top, far_bottom)], state)
    return attended[None], conv_out[None]


def solution(mesh):
    return jax.shard_map(
        body,
        mesh=mesh,
        in_specs=(
            P("fsdp", "ctx", None),
            P("fsdp", "ctx", None),
            P("fsdp", "ctx", None),
            P(),
            P("fsdp", None),
            P(),
            P(),
            P("fsdp", None),
            P("fsdp", "ctx"),
        ),
        out_specs=(P("fsdp", "ctx", None), P("fsdp", "ctx", None)),
        check_vma=False,
    )
```

```python
import functools
import math

import jax
import jax.numpy as jnp
import numpy as np
from jax import lax
from jax.experimental import pallas as pl
from jax.experimental.pallas import tpu as pltpu
from jax.sharding import PartitionSpec as P

HEAD = 128
TAPS = 4
EPISODES = 8
AXES = ("ctx", "fsdp")
CTX, FSDP = 8, 16
DEVICES = CTX * FSDP
MIB = 1 << 20


def place(i):
    c, f = divmod(i, FSDP)
    x, zl = divmod(c, 2)
    y, r = divmod(f, 4)
    zh, k = divmod(r, 2)
    return x, y, zh, zl, k


def device(x, y, zh, zl, k):
    return ((x % 4) * 2 + zl) * FSDP + ((y % 4) * 2 + zh) * 2 + k


def lead_core(x, zl):
    return (x + zl) % 2


def neighbour(x, y, zh, zl, way):
    return {
        "x+": (x + 1, y, zh, zl),
        "x-": (x - 1, y, zh, zl),
        "y+": (x, y + 1, zh, zl),
        "y-": (x, y - 1, zh, zl),
        "zlo": (x, y, zh, 1 - zl),
        "zhi": (x, y, 1 - zh, 1 - zl),
    }[way]


STEPS = (
    ((0, "y-", 0), (1, "zhi", 1)),
    ((0, "y+", 1),),
    ((0, "x-", 1), (1, "zlo", 0)),
    ((0, "y-", 0), (1, "y+", 1)),
    ((0, "zhi", 0), (1, "x+", 1)),
    ((0, "x-", 0), (1, "x+", 1)),
    ((0, "y-", 1), (1, "y+", 0)),
    ((0, "zlo", 0),),
)
SENT = ((0, 0), (0, 0), (1, 1), (1, 1), (1, 2), (4, 4), (5, 4), (5, 5))
SLOT_STEPS = ((0, 0), (1, 1), (3, 3), (4, 4), (5, 5), (6, 6), (7, 7), (8, 2))


def role_of(i):
    x, _, _, zl, k = place(i)
    return 0 if k == lead_core(x, zl) else 1


def weight_plan():
    pairs, held = [], [[i % FSDP for i in range(DEVICES)]]
    for step, sent in zip(STEPS, SENT):
        now, got = [], [-1] * DEVICES
        for i in range(DEVICES):
            for sender, way, receiver in step:
                if sender == role_of(i):
                    nx, ny, nzh, nzl = neighbour(*place(i)[:4], way)
                    lead = lead_core(nx, nzl)
                    to = device(nx, ny, nzh, nzl, lead if receiver == 0 else 1 - lead)
                    now.append((i, to))
                    got[to] = held[sent[role_of(i)]][i]
        pairs.append(now)
        held.append(got)
    slots = [[held[step[role_of(i)]][i] for step in SLOT_STEPS] for i in range(DEVICES)]
    return pairs, np.asarray(slots, np.int32)


WEIGHT_PAIRS, SLOTS = weight_plan()


def moved(way, wanted):
    pairs = [(i, device(*neighbour(*place(i)[:4], way), place(i)[4])) for i in range(DEVICES)]
    return [(i, to) for i, to in pairs if wanted(place(to)[0], place(to)[3])]


SWAP = [(i, i ^ 1) for i in range(DEVICES)]


def send(x, pairs):
    return lax.ppermute(x, AXES, pairs)


def together(*values):
    return lax.optimization_barrier(values)


def params(mib, **kw):
    return pltpu.CompilerParams(vmem_limit_bytes=mib * MIB, **kw)


WHOLE = pl.BlockSpec(memory_space=pltpu.VMEM)
SCALARS = pl.BlockSpec(memory_space=pltpu.SMEM)
ANYWHERE = pl.BlockSpec(memory_space=pl.ANY)
ROWS_HERE = 2
BLOCKS = 8
BASES = 1 + ROWS_HERE * EPISODES
LEAD = BASES + BLOCKS
CORE = LEAD + 1


def in_smem(scalars):
    return pltpu.with_memory_space_constraint(scalars, pltpu.SMEM)


SHORT = pl.CostEstimate(flops=1024, bytes_accessed=1024, transcendentals=0)


def norm_kernel(slots, h_ref, g_ref, mine_ref, other_ref, *, width, chunk, count):
    rows = h_ref.shape[0]
    here = pl.ds(pl.multiple_of(pl.program_id(0) * rows, rows), rows)
    total = jnp.zeros((rows, chunk), jnp.float32)
    for c in range(width // chunk):
        f = h_ref[:, c * chunk : (c + 1) * chunk].astype(jnp.float32)
        total = total + f * f
    mean = jnp.sum(total, axis=-1, keepdims=True) * (1.0 / width)
    factor = lax.rsqrt(mean + 1e-06)
    for which, out in ((1, other_ref), (0, mine_ref)):
        for s in range(count):
            at = pl.multiple_of(slots[which, s] * chunk, chunk)
            f = h_ref[:, pl.ds(at, chunk)].astype(jnp.float32)
            out[s, here, :] = (f * factor * g_ref[:, pl.ds(at, chunk)]).astype(jnp.bfloat16)


def norm(slots, hidden, gain, chunk):
    rows, width = hidden.shape
    count = slots.shape[1]
    tile = 64
    shape = pltpu.VMEM((count, rows, chunk), jnp.bfloat16)
    return pl.pallas_call(
        functools.partial(norm_kernel, width=width, chunk=chunk, count=count),
        grid=(rows // tile,),
        in_specs=[
            pl.BlockSpec(memory_space=pltpu.SMEM),
            pl.BlockSpec((tile, width), lambda i: (i, 0)),
            pl.BlockSpec((1, width), lambda i: (0, 0)),
        ],
        out_specs=[WHOLE, WHOLE],
        out_shape=[shape, shape],
        compiler_params=params(16),
        cost_estimate=SHORT,
        name="norm",
    )(slots, pltpu.with_memory_space_constraint(hidden, pltpu.HBM), gain)


def project_kernel(*refs, sides, slots, carried, after):
    del after
    count = len(slots)
    xs, ws = refs[:sides], refs[sides : sides + count]
    olds, outs = refs[sides + count :][:carried], refs[-sides:]
    tile = 256
    for s in range(count):
        for c in range(0, ws[s].shape[1], tile):
            cols = slice(c, c + tile)
            w = ws[s][:, cols]
            for side in range(sides):
                part = jnp.dot(xs[side][slots[s]], w, preferred_element_type=jnp.float32)
                if s:
                    part = outs[side][:, cols] + part
                elif carried:
                    part = olds[side][:, cols] + part
                outs[side][:, cols] = part


def project(xs, slots, weights, carried=(), after=()):
    _, rows, depth = xs[0].shape
    columns = weights[0].shape[1]
    sides = len(xs)
    inside = [
        pltpu.with_memory_space_constraint(v, pltpu.VMEM) for v in (*xs, *weights, *carried, *after)
    ]
    return pl.pallas_call(
        functools.partial(
            project_kernel, sides=sides, slots=slots, carried=len(carried), after=len(after)
        ),
        in_specs=[WHOLE] * len(inside),
        out_specs=[WHOLE] * sides,
        out_shape=[pltpu.VMEM((rows, columns), jnp.float32)] * sides,
        compiler_params=params(8),
        cost_estimate=SHORT,
        name="project",
    )(*inside)


def pick_kernel(flag_ref, a_ref, b_ref, o_ref):
    o_ref[...] = jnp.where(flag_ref[0:1, :] > 0, a_ref[...], b_ref[...])


def pick(flag, a, b):
    inside = [pltpu.with_memory_space_constraint(v, pltpu.VMEM) for v in (flag, a, b)]
    return pl.pallas_call(
        pick_kernel,
        in_specs=[WHOLE] * 3,
        out_specs=WHOLE,
        out_shape=pltpu.VMEM(a.shape, a.dtype),
        compiler_params=params(8),
        cost_estimate=SHORT,
        name="pick",
    )(*inside)


def finish_kernel(scalars, x0, x1, old0, old1, *refs, slots, counts, own):
    ws, out = refs[:-1], refs[-1]
    rows, tile = old0.shape[0], out.shape[1] // 2
    core = scalars[CORE] if own else 1 - scalars[CORE]
    for part in range(2):
        cols = pl.ds(pl.multiple_of((2 * part + core) * tile, tile), tile)
        for side, (x, old) in enumerate(((x0, old0), (x1, old1))):
            total = old[:, cols]
            at = 0
            for s, n in enumerate(counts):
                w = ws[at][:, cols]
                if n == 2:
                    w = jnp.where(scalars[LEAD] > 0, w, ws[at + 1][:, cols])
                total = total + jnp.dot(x[slots[s]], w, preferred_element_type=jnp.float32)
                at += n
            out[side * rows : (side + 1) * rows, part * tile : (part + 1) * tile] = total


def finish(scalars, xs, olds, slots, weights, own):
    weights = [w if isinstance(w, tuple) else (w,) for w in weights]
    counts = tuple(len(w) for w in weights)
    flat = [v for w in weights for v in w]
    rows, columns = olds[0].shape
    inside = [pltpu.with_memory_space_constraint(v, pltpu.VMEM) for v in (*xs, *olds, *flat)]
    depth = xs[0].shape[2]
    return pl.pallas_call(
        functools.partial(finish_kernel, slots=slots, counts=counts, own=own),
        in_specs=[SCALARS] + [WHOLE] * len(inside),
        out_specs=WHOLE,
        out_shape=pltpu.VMEM((2 * rows, columns // 2), jnp.float32),
        compiler_params=params(8),
        cost_estimate=SHORT,
        name="finish",
    )(in_smem(scalars), *inside)


def add_kernel(a_ref, b_ref, o_ref):
    o_ref[...] = (a_ref[...] + b_ref[...]).astype(o_ref.dtype)


def add(a, b):
    inside = [pltpu.with_memory_space_constraint(v, pltpu.VMEM) for v in (a, b)]
    return pl.pallas_call(
        add_kernel,
        in_specs=[WHOLE, WHOLE],
        out_specs=WHOLE,
        out_shape=pltpu.VMEM(a.shape, jnp.bfloat16),
        compiler_params=params(8),
        cost_estimate=SHORT,
        name="add",
    )(*inside)


PIECES = 8


def copies_of(pairs, sems):
    copies = []
    for i, (source, target, rows) in enumerate(pairs):
        step = rows // PIECES
        for p in range(PIECES):
            here = pl.ds(p * step, step)
            copies.append(pltpu.make_async_copy(source(here), target(here), sems.at[i, p]))
    return copies


def split_kernel(scalars, q_ref, out_ref, sems):
    rows, width = out_ref.shape
    cols = pl.ds(pl.multiple_of((1 - scalars[CORE]) * width, width), width)
    copies = copies_of([(lambda r: q_ref.at[r, cols], lambda r: out_ref.at[r, :], rows)], sems)
    for c in copies:
        c.start()
    for c in copies:
        c.wait()


def split(scalars, queries):
    rows, width = queries.shape
    return pl.pallas_call(
        split_kernel,
        in_specs=[SCALARS, ANYWHERE],
        out_specs=WHOLE,
        out_shape=pltpu.VMEM((rows, width // 2), queries.dtype),
        scratch_shapes=[pltpu.SemaphoreType.DMA((1, PIECES))],
        compiler_params=params(8),
        cost_estimate=SHORT,
        name="split",
    )(in_smem(scalars), pltpu.with_memory_space_constraint(queries, pltpu.HBM))


def merge_kernel(scalars, part_ref, all_in, all_ref, sems):
    del all_in
    rows, width = part_ref.shape
    cols = pl.ds(pl.multiple_of((1 - scalars[CORE]) * width, width), width)
    copies = copies_of(
        [(lambda r: part_ref.at[r, :], lambda r: all_ref.at[r, cols], rows)], sems
    )
    for c in copies:
        c.start()
    for c in copies:
        c.wait()


def merge(scalars, part, whole):
    return pl.pallas_call(
        merge_kernel,
        in_specs=[SCALARS, WHOLE, ANYWHERE],
        out_specs=ANYWHERE,
        out_shape=jax.ShapeDtypeStruct(whole.shape, whole.dtype),
        input_output_aliases={2: 0},
        scratch_shapes=[pltpu.SemaphoreType.DMA((1, PIECES))],
        compiler_params=params(8),
        cost_estimate=SHORT,
        name="merge",
    )(in_smem(scalars), pltpu.with_memory_space_constraint(part, pltpu.VMEM), whole)


def conv_kernel(info, x_ref, halo_ref, w_ref, b_ref, o_ref, token, pick, before):
    rows, width = x_ref.shape
    ahead = halo_ref.shape[0]
    token[...] = jnp.zeros_like(token)

    @pl.when(pl.program_id(0) == 0)
    def _():
        before[...] = halo_ref[...]

    shape = (rows, ahead + rows)
    pos = info[0] + pl.program_id(0) * rows + lax.broadcasted_iota(jnp.int32, shape, 0)
    begin = jnp.zeros(shape, jnp.int32)
    for e in range(EPISODES):
        begin = jnp.where(info[1 + e] <= pos, jnp.maximum(begin, info[1 + e]), begin)
    apart = lax.broadcasted_iota(jnp.int32, shape, 0) + ahead - lax.broadcasted_iota(jnp.int32, shape, 1)
    for tap in range(TAPS):
        behind = TAPS - 1 - tap
        taken = (apart == behind) & (pos - behind >= begin)
        pick[tap * rows : (tap + 1) * rows, :] = jnp.where(taken, 1.0, 0.0).astype(pick.dtype)

    lanes = 256
    for c in range(0, width, lanes):
        cols = slice(c, c + lanes)
        source = jnp.concatenate([before[:, cols], x_ref[:, cols]], axis=0)
        taps = jnp.dot(pick[...], source, preferred_element_type=jnp.float32)
        mixing = b_ref[:, cols] + taps[:rows] * w_ref[0:1, cols]
        for tap in range(1, TAPS):
            mixing = mixing + taps[tap * rows : (tap + 1) * rows] * w_ref[tap : tap + 1, cols]
        by_half = 0.5 * mixing
        o_ref[:, cols] = (by_half + by_half * jnp.tanh(by_half)).astype(o_ref.dtype)
    before[...] = x_ref[rows - ahead :, :]


def conv(info, x, halo, weight, bias):
    rows, width = x.shape
    tile = 64
    ahead = halo.shape[0]
    full = lambda n: pl.BlockSpec((n, width), lambda i: (0, 0))
    return pl.pallas_call(
        conv_kernel,
        grid=(rows // tile,),
        in_specs=[
            SCALARS,
            pl.BlockSpec((tile, width), lambda i: (i, 0)),
            full(ahead),
            full(TAPS),
            full(1),
        ],
        out_specs=[pl.BlockSpec((tile, width), lambda i: (i, 0)), WHOLE],
        out_shape=[
            jax.ShapeDtypeStruct((rows, width), x.dtype),
            pltpu.VMEM((8, 128), jnp.float32),
        ],
        scratch_shapes=[
            pltpu.VMEM((TAPS * tile, ahead + tile), jnp.bfloat16),
            pltpu.VMEM((ahead, width), x.dtype),
        ],
        compiler_params=params(16),
        cost_estimate=SHORT,
        name="conv",
    )(in_smem(info), x, halo, weight, bias)


def attend_kernel(info, *refs, count, per_group, stage, at, row):
    if stage == "first":
        q1_ref, *refs = refs
    else:
        q0_ref, q1_ref, *refs = refs
    ks, vs = refs[:count], refs[count : 2 * count]
    rest = refs[2 * count :]
    if stage == "first":
        q_hbm, m_ref, a_ref, own_ref, q_ref, mask_ref, q_sems = rest
        m_in, a_in = m_ref, a_ref
    elif stage == "middle":
        m_in, a_in, m_ref, a_ref, q_ref, mask_ref = rest
    elif row:
        m_in, a_in, o_ref, q_ref, mask_ref = rest
    else:
        m_in, a_in, o_hbm, q_ref, mask_ref, o_buf, sems = rest
    rows, keys = mask_ref.shape[1:]
    factor = math.log2(math.e) / math.sqrt(HEAD)
    first = info[0]
    if stage == "last":
        here, group = row, pl.program_id(0)
        q_ref = q1_ref if row else q0_ref
    else:
        here, group = 1 - pl.program_id(0) // 2, pl.program_id(0) % 2
    if stage == "middle":
        q_ref[...] = jnp.where(here == 0, q0_ref[...], q1_ref[...])
    if stage == "first":
        width = own_ref.shape[1]
        cols = pl.ds(pl.multiple_of(info[CORE] * width, width), width)
        copies = copies_of(
            [(lambda r: q_hbm.at[r, cols], lambda r: own_ref.at[r, :], own_ref.shape[0])], q_sems
        )

        @pl.when(pl.program_id(0) == 0)
        def _():
            for c in copies:
                c.start()

        @pl.when(pl.program_id(0) == 2)
        def _():
            for c in copies:
                c.wait()

        @pl.when(here == 0)
        def _():
            part = q_ref.shape[1]
            q_ref[...] = own_ref[:, pl.ds(pl.multiple_of(group * part, part), part)]

        @pl.when(here == 1)
        def _():
            q_ref[...] = q1_ref[...]

    if stage == "last" and not row:
        o_ref = o_buf.at[group]

    def start(e):
        return info[1 + here * EPISODES + e]

    lowest = jnp.int32(0)
    for e in range(EPISODES):
        lowest = jnp.where(start(e) <= first, jnp.maximum(lowest, start(e)), lowest)
    head = (here * 2 + group) * per_group

    def divided(h, a):
        value = (a[:, :HEAD] / a[:, HEAD:]).astype(jnp.bfloat16)
        if row:
            part = per_group * HEAD
            at_column = pl.multiple_of(group * part, part) + h * HEAD
            o_ref[:, pl.ds(pl.multiple_of(at_column, HEAD), HEAD)] = value
        else:
            o_ref[:, h * HEAD : (h + 1) * HEAD] = value

    def work(some):
        pos = first + lax.broadcasted_iota(jnp.int32, (rows, keys), 0)
        begin = jnp.zeros((rows, keys), jnp.int32)
        for e in range(EPISODES):
            begin = jnp.where(start(e) <= pos, jnp.maximum(begin, start(e)), begin)
        for b in some:
            key_pos = info[BASES + at + b] + lax.broadcasted_iota(jnp.int32, (rows, keys), 1)
            allowed = (key_pos >= begin) & (key_pos <= pos)
            mask_ref[b] = jnp.where(allowed, 0.0, -1e30)
        k = [ks[b][...] for b in some]
        v = [jnp.concatenate([vs[b][...], jnp.ones((keys, HEAD), jnp.bfloat16)], axis=1) for b in some]
        for h in range(per_group):
            q = q_ref[:, h * HEAD : (h + 1) * HEAD]
            scores = [
                lax.dot_general(q, k_b, (((1,), (1,)), ((), ())), preferred_element_type=jnp.float32)
                + mask_ref[b]
                for b, k_b in zip(some, k)
            ]
            top = scores[0]
            for s in scores[1:]:
                top = jnp.maximum(top, s)
            top = jnp.max(top, axis=1, keepdims=True)
            if stage == "first":
                new = jnp.broadcast_to(top, (rows, HEAD))
                a = None
            else:
                old = m_in[head + h]
                new = jnp.maximum(old, top)
                shrink = jnp.exp2((old - new) * factor)
                a = a_in[head + h] * jnp.concatenate([shrink, shrink], axis=1)
            wide = jnp.concatenate([new] * (keys // HEAD), axis=1)
            for s, v_b in zip(scores, v):
                w = jnp.exp2((s - wide) * factor).astype(jnp.bfloat16)
                part = jnp.dot(w, v_b, preferred_element_type=jnp.float32)
                a = part if a is None else a + part
            if stage == "last":
                divided(h, a)
            else:
                a_ref[head + h] = a
                m_ref[head + h] = new

    if stage == "first":
        work([0])
    else:
        lives = []
        for b in range(count):
            base = info[BASES + at + b]
            lives.append((base < first) & (base + keys > lowest))
        done = functools.reduce(jnp.logical_and, lives)
        pl.when(done)(functools.partial(work, list(range(count))))
        if count > 2:
            pair = lives[0] & lives[1] & jnp.logical_not(done)
            pl.when(pair)(functools.partial(work, [0, 1]))
            done = done | pair
        if count > 1:
            for b in range(count):
                pl.when(lives[b] & jnp.logical_not(done))(functools.partial(work, [b]))
        if stage == "last":

            @pl.when(jnp.logical_not(done))
            def _():
                for h in range(per_group):
                    divided(h, a_in[head + h])

    if stage == "last" and not row:
        width = o_buf.shape[2]

        def out_copy(j):
            cols = pl.ds(pl.multiple_of((info[CORE] * 2 + j) * width, width), width)
            return pltpu.make_async_copy(o_buf.at[j], o_hbm.at[:, cols], sems.at[j])

        out_copy(group).start()

        @pl.when(group == 1)
        def _():
            out_copy(0).wait()
            out_copy(1).wait()


def attend(stage, scalars, at, queries, blocks, state=(), row=None, whole=None):
    rows, width = queries[0].shape
    columns = blocks[0].shape[1]
    keys = blocks[0].shape[0] // (1 if stage == "last" else ROWS_HERE)
    count = len(blocks)
    group = width // 2
    heads = ROWS_HERE * width // HEAD
    scratch = [pltpu.VMEM((rows, group), jnp.bfloat16), pltpu.VMEM((count, rows, keys), jnp.float32)]
    half_columns = columns // (2 * HEAD)
    if stage == "last":
        grid = (2,)
        q_specs = [pl.BlockSpec((rows, group), lambda g: (0, g))] * 2
        k_spec = pl.BlockSpec((keys, HEAD), lambda g: (0, g))
        v_spec = pl.BlockSpec((keys, HEAD), lambda g: (0, half_columns + g))
        if row:
            out_shape = pltpu.VMEM((rows, width), jnp.bfloat16)
            out_specs = WHOLE
        else:
            out_shape = jax.ShapeDtypeStruct((rows, 2 * width), jnp.bfloat16)
            out_specs = ANYWHERE
            scratch += [pltpu.VMEM((2, rows, group), jnp.bfloat16), pltpu.SemaphoreType.DMA((2,))]
    else:
        grid = (4,)
        q_specs = [pl.BlockSpec((rows, group), lambda g: (0, g % 2))] * 2
        k_spec = pl.BlockSpec((keys, HEAD), lambda g: (1 - g // 2, g % 2))
        v_spec = pl.BlockSpec((keys, HEAD), lambda g: (1 - g // 2, half_columns + g % 2))
        out_shape = [
            pltpu.VMEM((heads, rows, HEAD), jnp.float32),
            pltpu.VMEM((heads, rows, 2 * HEAD), jnp.float32),
        ]
        out_specs = [WHOLE, WHOLE]
        if stage == "first":
            out_shape.append(pltpu.VMEM((rows, width), jnp.bfloat16))
            out_specs.append(WHOLE)
            scratch.append(pltpu.SemaphoreType.DMA((1, PIECES)))
            q_specs = q_specs[1:]
    in_specs = [SCALARS] + q_specs + [k_spec] * count + [v_spec] * count + [WHOLE] * len(state)
    extra = []
    if stage == "first":
        in_specs.append(ANYWHERE)
        extra = [pltpu.with_memory_space_constraint(whole, pltpu.HBM)]
    aliases = {} if stage != "middle" else {len(in_specs) - 2: 0, len(in_specs) - 1: 1}
    state = [pltpu.with_memory_space_constraint(v, pltpu.VMEM) for v in state]
    return pl.pallas_call(
        functools.partial(
            attend_kernel, count=count, per_group=group // HEAD, stage=stage, at=at, row=row
        ),
        grid=grid,
        in_specs=in_specs,
        out_specs=out_specs,
        out_shape=out_shape,
        input_output_aliases=aliases,
        scratch_shapes=scratch,
        compiler_params=params(14),
        cost_estimate=SHORT,
        name="attend_" + stage,
    )(in_smem(scalars), *queries, *blocks, *blocks, *state, *extra)


def body(
    hidden, queries, conv_input, norm_gain, kv_weight, conv_weight, conv_bias, starts, segment_ids
):
    del segment_ids
    rows = hidden.shape[1]
    ctx = lax.axis_index("ctx")
    me = ctx * FSDP + lax.axis_index("fsdp")
    x, zl = ctx // 2, ctx % 2
    depth = kv_weight.shape[0]
    leads = lax.axis_index("fsdp") % 2 == lead_core(x, zl)
    table = jnp.asarray(SLOTS)
    slots = jnp.stack([table[me], table[me ^ 1]])

    def base(dx, dz):
        return (((x + dx) % 4) * 2 + (zl + dz) % 2) * rows

    bases = [base(0, 0), base(0, 1), base(-1, 0), base(1, 0), base(-1, 1), base(2, 0), base(1, 1), base(2, 1)]
    core = lax.axis_index("fsdp") % 2
    flags = jnp.stack([leads.astype(jnp.int32), core])
    scalars = jnp.concatenate(
        [(ctx * rows)[None], starts[0], send(starts, SWAP)[0], jnp.stack(bases), flags]
    )
    signal = conv_input[0]
    tail = signal[rows - 16 :]
    flag = jnp.full((8, kv_weight.shape[1]), leads.astype(jnp.int32))
    slots, tail, scalars, flag = together(slots, tail, scalars, flag)

    w0 = kv_weight
    w1 = send(w0, WEIGHT_PAIRS[0])
    w2 = send(w0, WEIGHT_PAIRS[1])
    halo = lax.ppermute(tail, "ctx", [(i, i + 1) for i in range(CTX - 1)])
    mine, other = norm(slots, hidden[0], norm_gain[None], depth)
    w1, w2, halo, mine, other, scalars, flag = together(w1, w2, halo, mine, other, scalars, flag)

    w4 = send(w1, WEIGHT_PAIRS[3])
    theirs = send(other, SWAP)
    w5 = send(pick(flag, w1, w2), WEIGHT_PAIRS[4])
    theirs, scalars_later, w1_later = together(theirs, scalars, w1)
    w3 = send(w1_later, WEIGHT_PAIRS[2])
    q_theirs = send(split(scalars_later, queries[0]), SWAP)
    sums = project((mine, theirs), (0, 1), (w0, w1))

    w4, w5, q_theirs, *sums = together(w4, w5, q_theirs, *sums)
    w6 = send(w4, WEIGHT_PAIRS[5])
    w7 = send(pick(flag, w5, w4), WEIGHT_PAIRS[6])
    w8 = send(w5, WEIGHT_PAIRS[7])
    conv_out, token = conv(scalars, signal, halo, conv_weight, conv_bias[None])
    sums = project((mine, theirs), (2, 3, 4), (w3, w4, w5), sums, (token,))

    last = ((5, 6, 7), (w6, w7, (w8, w2)))
    their_sum = finish(scalars, (theirs, mine), sums[::-1], *last, False)
    back = send(their_sum, SWAP)
    my_sum = finish(scalars, (mine, theirs), sums, *last, True)
    kv = add(my_sum, back)

    right_end = (0, 3)
    from_right = send(kv, moved("x-", lambda x, z: x in right_end))
    from_pair = send(kv, moved("zlo", lambda x, z: x < 3 or z == 1))
    from_left = send(kv, moved("x+", lambda x, z: x > 0))
    *state, q_mine = attend("first", scalars, 0, (q_theirs,), [kv], whole=queries[0])
    q = (q_mine, q_theirs)
    from_right, from_pair, *state = together(from_right, from_pair, *state)
    left_pair = send(from_pair, moved("x+", lambda x, z: x > 0))
    right_pair = send(from_right, moved("zlo", lambda x, z: x in right_end))
    far = send(from_right, moved("x-", lambda x, z: x > 1))
    state = attend("middle", scalars, 1, q, [from_pair, from_left, from_right], state)
    left_pair, right_pair, *state = together(left_pair, right_pair, *state)
    far_own = send(left_pair[:rows], moved("x+", lambda x, z: x > 1))
    far_other = send(right_pair[rows:], moved("x-", lambda x, z: x > 1))
    state = attend("middle", scalars, 4, q, [left_pair, far, right_pair], state)
    far_own, far_other, *state = together(far_own, far_other, *state)
    for_other = attend("last", scalars, 7, q, [far_other], state, row=1)
    from_other = send(for_other, SWAP)
    attended = attend("last", scalars, 7, q, [far_own], state, row=0)
    attended = merge(scalars, from_other, attended)
    return attended[None], conv_out[None]


def solution(mesh):
    return jax.shard_map(
        body,
        mesh=mesh,
        in_specs=(
            P("fsdp", "ctx", None),
            P("fsdp", "ctx", None),
            P("fsdp", "ctx", None),
            P(),
            P("fsdp", None),
            P(),
            P(),
            P("fsdp", None),
            P("fsdp", "ctx"),
        ),
        out_specs=(P("fsdp", "ctx", None), P("fsdp", "ctx", None)),
        check_vma=False,
    )
```

```python
import functools
import math

import jax
import jax.numpy as jnp
import numpy as np
from jax import lax
from jax.experimental import pallas as pl
from jax.experimental.pallas import tpu as pltpu
from jax.sharding import PartitionSpec as P

HEAD = 128
TAPS = 4
EPISODES = 8
AXES = ("ctx", "fsdp")
CTX, FSDP = 8, 16
DEVICES = CTX * FSDP
MIB = 1 << 20


def place(i):
    c, f = divmod(i, FSDP)
    x, zl = divmod(c, 2)
    y, r = divmod(f, 4)
    zh, k = divmod(r, 2)
    return x, y, zh, zl, k


def device(x, y, zh, zl, k):
    return ((x % 4) * 2 + zl) * FSDP + ((y % 4) * 2 + zh) * 2 + k


def lead_core(x, zl):
    return (x + zl) % 2


def neighbour(x, y, zh, zl, way):
    return {
        "x+": (x + 1, y, zh, zl),
        "x-": (x - 1, y, zh, zl),
        "y+": (x, y + 1, zh, zl),
        "y-": (x, y - 1, zh, zl),
        "zlo": (x, y, zh, 1 - zl),
        "zhi": (x, y, 1 - zh, 1 - zl),
    }[way]


STEPS = (
    ((0, "y-", 0), (1, "zhi", 1)),
    ((0, "y+", 1),),
    ((0, "x-", 1), (1, "zlo", 0)),
    ((0, "y-", 0), (1, "y+", 1)),
    ((0, "zhi", 0), (1, "x+", 1)),
    ((0, "x-", 0), (1, "x+", 1)),
    ((0, "y-", 1), (1, "y+", 0)),
    ((0, "zlo", 0),),
)
SENT = ((0, 0), (0, 0), (1, 1), (1, 1), (1, 2), (4, 4), (5, 4), (5, 5))
SLOT_STEPS = ((0, 0), (1, 1), (3, 3), (4, 4), (5, 5), (6, 6), (7, 7), (8, 2))


def role_of(i):
    x, _, _, zl, k = place(i)
    return 0 if k == lead_core(x, zl) else 1


def weight_plan():
    pairs, held = [], [[i % FSDP for i in range(DEVICES)]]
    for step, sent in zip(STEPS, SENT):
        now, got = [], [-1] * DEVICES
        for i in range(DEVICES):
            for sender, way, receiver in step:
                if sender == role_of(i):
                    nx, ny, nzh, nzl = neighbour(*place(i)[:4], way)
                    lead = lead_core(nx, nzl)
                    to = device(nx, ny, nzh, nzl, lead if receiver == 0 else 1 - lead)
                    now.append((i, to))
                    got[to] = held[sent[role_of(i)]][i]
        pairs.append(now)
        held.append(got)
    slots = [[held[step[role_of(i)]][i] for step in SLOT_STEPS] for i in range(DEVICES)]
    return pairs, np.asarray(slots, np.int32)


WEIGHT_PAIRS, SLOTS = weight_plan()


def moved(way, wanted):
    pairs = [(i, device(*neighbour(*place(i)[:4], way), place(i)[4])) for i in range(DEVICES)]
    return [(i, to) for i, to in pairs if wanted(place(to)[0], place(to)[3])]


SWAP = [(i, i ^ 1) for i in range(DEVICES)]


def send(x, pairs):
    return lax.ppermute(x, AXES, pairs)


def together(*values):
    return lax.optimization_barrier(values)


def params(mib, **kw):
    return pltpu.CompilerParams(vmem_limit_bytes=mib * MIB, **kw)


WHOLE = pl.BlockSpec(memory_space=pltpu.VMEM)
SCALARS = pl.BlockSpec(memory_space=pltpu.SMEM)
ANYWHERE = pl.BlockSpec(memory_space=pl.ANY)
ROWS_HERE = 2
BLOCKS = 8
BASES = 1 + ROWS_HERE * EPISODES
LEAD = BASES + BLOCKS
CORE = LEAD + 1


def in_smem(scalars):
    return pltpu.with_memory_space_constraint(scalars, pltpu.SMEM)


SHORT = pl.CostEstimate(flops=1024, bytes_accessed=1024, transcendentals=0)


def norm_kernel(slots, h_ref, g_ref, mine_ref, other_ref, *, width, chunk, count):
    rows = h_ref.shape[0]
    here = pl.ds(pl.multiple_of(pl.program_id(0) * rows, rows), rows)
    total = jnp.zeros((rows, chunk), jnp.float32)
    for c in range(width // chunk):
        f = h_ref[:, c * chunk : (c + 1) * chunk].astype(jnp.float32)
        total = total + f * f
    mean = jnp.sum(total, axis=-1, keepdims=True) * (1.0 / width)
    factor = lax.rsqrt(mean + 1e-06)
    for which, out in ((1, other_ref), (0, mine_ref)):
        for s in range(count):
            at = pl.multiple_of(slots[which, s] * chunk, chunk)
            f = h_ref[:, pl.ds(at, chunk)].astype(jnp.float32)
            out[s, here, :] = (f * factor * g_ref[:, pl.ds(at, chunk)]).astype(jnp.bfloat16)


def norm(slots, hidden, gain, chunk):
    rows, width = hidden.shape
    count = slots.shape[1]
    tile = 64
    shape = pltpu.VMEM((count, rows, chunk), jnp.bfloat16)
    return pl.pallas_call(
        functools.partial(norm_kernel, width=width, chunk=chunk, count=count),
        grid=(rows // tile,),
        in_specs=[
            pl.BlockSpec(memory_space=pltpu.SMEM),
            pl.BlockSpec((tile, width), lambda i: (i, 0)),
            pl.BlockSpec((1, width), lambda i: (0, 0)),
        ],
        out_specs=[WHOLE, WHOLE],
        out_shape=[shape, shape],
        compiler_params=params(16),
        cost_estimate=SHORT,
        name="norm",
    )(slots, pltpu.with_memory_space_constraint(hidden, pltpu.HBM), gain)


def project_kernel(*refs, sides, slots, carried, after):
    del after
    count = len(slots)
    xs, ws = refs[:sides], refs[sides : sides + count]
    olds, outs = refs[sides + count :][:carried], refs[-sides:]
    tile = 256
    for s in range(count):
        for c in range(0, ws[s].shape[1], tile):
            cols = slice(c, c + tile)
            w = ws[s][:, cols]
            for side in range(sides):
                part = jnp.dot(xs[side][slots[s]], w, preferred_element_type=jnp.float32)
                if s:
                    part = outs[side][:, cols] + part
                elif carried:
                    part = olds[side][:, cols] + part
                outs[side][:, cols] = part


def project(xs, slots, weights, carried=(), after=()):
    _, rows, depth = xs[0].shape
    columns = weights[0].shape[1]
    sides = len(xs)
    inside = [
        pltpu.with_memory_space_constraint(v, pltpu.VMEM) for v in (*xs, *weights, *carried, *after)
    ]
    return pl.pallas_call(
        functools.partial(
            project_kernel, sides=sides, slots=slots, carried=len(carried), after=len(after)
        ),
        in_specs=[WHOLE] * len(inside),
        out_specs=[WHOLE] * sides,
        out_shape=[pltpu.VMEM((rows, columns), jnp.float32)] * sides,
        compiler_params=params(8),
        cost_estimate=SHORT,
        name="project",
    )(*inside)


def pick_kernel(flag_ref, a_ref, b_ref, o_ref):
    o_ref[...] = jnp.where(flag_ref[0:1, :] > 0, a_ref[...], b_ref[...])


def pick(flag, a, b):
    inside = [pltpu.with_memory_space_constraint(v, pltpu.VMEM) for v in (flag, a, b)]
    return pl.pallas_call(
        pick_kernel,
        in_specs=[WHOLE] * 3,
        out_specs=WHOLE,
        out_shape=pltpu.VMEM(a.shape, a.dtype),
        compiler_params=params(8),
        cost_estimate=SHORT,
        name="pick",
    )(*inside)


def finish_kernel(scalars, x0, x1, old0, old1, *refs, slots, counts, own):
    ws, out = refs[:-1], refs[-1]
    rows, tile = old0.shape[0], out.shape[1] // 2
    core = scalars[CORE] if own else 1 - scalars[CORE]
    for part in range(2):
        cols = pl.ds(pl.multiple_of((2 * part + core) * tile, tile), tile)
        for side, (x, old) in enumerate(((x0, old0), (x1, old1))):
            total = old[:, cols]
            at = 0
            for s, n in enumerate(counts):
                w = ws[at][:, cols]
                if n == 2:
                    w = jnp.where(scalars[LEAD] > 0, w, ws[at + 1][:, cols])
                total = total + jnp.dot(x[slots[s]], w, preferred_element_type=jnp.float32)
                at += n
            out[side * rows : (side + 1) * rows, part * tile : (part + 1) * tile] = total


def finish(scalars, xs, olds, slots, weights, own):
    weights = [w if isinstance(w, tuple) else (w,) for w in weights]
    counts = tuple(len(w) for w in weights)
    flat = [v for w in weights for v in w]
    rows, columns = olds[0].shape
    inside = [pltpu.with_memory_space_constraint(v, pltpu.VMEM) for v in (*xs, *olds, *flat)]
    depth = xs[0].shape[2]
    return pl.pallas_call(
        functools.partial(finish_kernel, slots=slots, counts=counts, own=own),
        in_specs=[SCALARS] + [WHOLE] * len(inside),
        out_specs=WHOLE,
        out_shape=pltpu.VMEM((2 * rows, columns // 2), jnp.float32),
        compiler_params=params(8),
        cost_estimate=SHORT,
        name="finish",
    )(in_smem(scalars), *inside)


def add_kernel(a_ref, b_ref, o_ref):
    o_ref[...] = (a_ref[...] + b_ref[...]).astype(o_ref.dtype)


def add(a, b):
    inside = [pltpu.with_memory_space_constraint(v, pltpu.VMEM) for v in (a, b)]
    return pl.pallas_call(
        add_kernel,
        in_specs=[WHOLE, WHOLE],
        out_specs=WHOLE,
        out_shape=pltpu.VMEM(a.shape, jnp.bfloat16),
        compiler_params=params(8),
        cost_estimate=SHORT,
        name="add",
    )(*inside)


PIECES = 8


def copies_of(pairs, sems):
    copies = []
    for i, (source, target, rows) in enumerate(pairs):
        step = rows // PIECES
        for p in range(PIECES):
            here = pl.ds(p * step, step)
            copies.append(pltpu.make_async_copy(source(here), target(here), sems.at[i, p]))
    return copies


def split_kernel(scalars, q_ref, out_ref, sems):
    rows, width = out_ref.shape
    cols = pl.ds(pl.multiple_of((1 - scalars[CORE]) * width, width), width)
    copies = copies_of([(lambda r: q_ref.at[r, cols], lambda r: out_ref.at[r, :], rows)], sems)
    for c in copies:
        c.start()
    for c in copies:
        c.wait()


def split(scalars, queries):
    rows, width = queries.shape
    return pl.pallas_call(
        split_kernel,
        in_specs=[SCALARS, ANYWHERE],
        out_specs=WHOLE,
        out_shape=pltpu.VMEM((rows, width // 2), queries.dtype),
        scratch_shapes=[pltpu.SemaphoreType.DMA((1, PIECES))],
        compiler_params=params(8),
        cost_estimate=SHORT,
        name="split",
    )(in_smem(scalars), pltpu.with_memory_space_constraint(queries, pltpu.HBM))


def conv_kernel(info, x_ref, halo_ref, w_ref, b_ref, o_ref, token, pick, before):
    rows, width = x_ref.shape
    ahead = halo_ref.shape[0]
    token[...] = jnp.zeros_like(token)

    @pl.when(pl.program_id(0) == 0)
    def _():
        before[...] = halo_ref[...]

    shape = (rows, ahead + rows)
    pos = info[0] + pl.program_id(0) * rows + lax.broadcasted_iota(jnp.int32, shape, 0)
    begin = jnp.zeros(shape, jnp.int32)
    for e in range(EPISODES):
        begin = jnp.where(info[1 + e] <= pos, jnp.maximum(begin, info[1 + e]), begin)
    apart = lax.broadcasted_iota(jnp.int32, shape, 0) + ahead - lax.broadcasted_iota(jnp.int32, shape, 1)
    for tap in range(TAPS):
        behind = TAPS - 1 - tap
        taken = (apart == behind) & (pos - behind >= begin)
        pick[tap * rows : (tap + 1) * rows, :] = jnp.where(taken, 1.0, 0.0).astype(pick.dtype)

    lanes = 256
    for c in range(0, width, lanes):
        cols = slice(c, c + lanes)
        source = jnp.concatenate([before[:, cols], x_ref[:, cols]], axis=0)
        taps = jnp.dot(pick[...], source, preferred_element_type=jnp.float32)
        mixing = b_ref[:, cols] + taps[:rows] * w_ref[0:1, cols]
        for tap in range(1, TAPS):
            mixing = mixing + taps[tap * rows : (tap + 1) * rows] * w_ref[tap : tap + 1, cols]
        by_half = 0.5 * mixing
        o_ref[:, cols] = (by_half + by_half * jnp.tanh(by_half)).astype(o_ref.dtype)
    before[...] = x_ref[rows - ahead :, :]


def conv(info, x, halo, weight, bias):
    rows, width = x.shape
    tile = 64
    ahead = halo.shape[0]
    full = lambda n: pl.BlockSpec((n, width), lambda i: (0, 0))
    return pl.pallas_call(
        conv_kernel,
        grid=(rows // tile,),
        in_specs=[
            SCALARS,
            pl.BlockSpec((tile, width), lambda i: (i, 0)),
            full(ahead),
            full(TAPS),
            full(1),
        ],
        out_specs=[pl.BlockSpec((tile, width), lambda i: (i, 0)), WHOLE],
        out_shape=[
            jax.ShapeDtypeStruct((rows, width), x.dtype),
            pltpu.VMEM((8, 128), jnp.float32),
        ],
        scratch_shapes=[
            pltpu.VMEM((TAPS * tile, ahead + tile), jnp.bfloat16),
            pltpu.VMEM((ahead, width), x.dtype),
        ],
        compiler_params=params(16),
        cost_estimate=SHORT,
        name="conv",
    )(in_smem(info), x, halo, weight, bias)


def attend_kernel(info, *refs, count, per_group, stage, at, row, part):
    if stage == "first":
        q1_ref, *refs = refs
    elif stage == "middle" and row is None:
        q0_ref, q1_ref, *refs = refs
    else:
        q_ref, *refs = refs
    ks, vs, rest = refs[:count], refs[count : 2 * count], refs[2 * count :]
    if stage == "first":
        q_hbm, m_ref, a_ref, own_ref, mask_ref, q_ref, q_sems = rest
    elif stage == "middle":
        m_in, a_in, m_ref, a_ref, mask_ref, *rest = rest
        if row is None:
            (q_ref,) = rest
    elif stage == "other":
        m_in, a_in, o_ref, mask_ref = rest
    elif count > 1:
        m_in, a_in, o_hbm, m_ref, a_ref, mask_ref, o_ref, sems = rest
    else:
        m_in, a_in, came_ref, _, o_hbm, mask_ref, o_ref, sems = rest
    rows, keys = mask_ref.shape[1:]
    factor = math.log2(math.e) / math.sqrt(HEAD)
    first = info[0]
    if row is None:
        here, group = 1 - pl.program_id(0) // 2, pl.program_id(0) % 2
    else:
        here, group = row, pl.program_id(0) if part is None else part
    if stage == "middle" and row is None:
        q_ref[...] = jnp.where(here == 0, q0_ref[...], q1_ref[...])
    if stage == "first":
        width = own_ref.shape[1]
        cols = pl.ds(pl.multiple_of(info[CORE] * width, width), width)
        copies = copies_of(
            [(lambda r: q_hbm.at[r, cols], lambda r: own_ref.at[r, :], own_ref.shape[0])], q_sems
        )

        @pl.when(pl.program_id(0) == 0)
        def _():
            for c in copies:
                c.start()

        @pl.when(pl.program_id(0) == 2)
        def _():
            for c in copies:
                c.wait()

        @pl.when(here == 0)
        def _():
            n = q_ref.shape[1]
            q_ref[...] = own_ref[:, pl.ds(pl.multiple_of(group * n, n), n)]

        @pl.when(here == 1)
        def _():
            q_ref[...] = q1_ref[...]

    if stage == "own":
        width = per_group * HEAD
        cols = pl.ds(pl.multiple_of((info[CORE] * 2 + part) * width, width), width)
        out_copies = copies_of(
            [(lambda r: o_ref.at[r, :], lambda r: o_hbm.at[r, cols], rows)], sems
        )
        came_copies = []
        if count == 1:
            wide_cols = pl.ds(
                pl.multiple_of((1 - info[CORE]) * 2 * width, 2 * width), 2 * width
            )
            came_copies = copies_of(
                [(lambda r: came_ref.at[r, :], lambda r: o_hbm.at[r, wide_cols], rows)],
                sems.at[1:2],
            )
        for c in came_copies:
            c.start()

    def start(e):
        return info[1 + here * EPISODES + e]

    lowest = jnp.int32(0)
    for e in range(EPISODES):
        lowest = jnp.where(start(e) <= first, jnp.maximum(lowest, start(e)), lowest)
    head = (here * 2 + group) * per_group

    def divided(h, a):
        value = (a[:, :HEAD] / a[:, HEAD:]).astype(jnp.bfloat16)
        if stage == "other":
            where = pl.multiple_of(group * per_group * HEAD, per_group * HEAD) + h * HEAD
            o_ref[:, pl.ds(pl.multiple_of(where, HEAD), HEAD)] = value
        else:
            o_ref[:, h * HEAD : (h + 1) * HEAD] = value

    def work(some, final=stage in ("own", "other")):
        pos = first + lax.broadcasted_iota(jnp.int32, (rows, keys), 0)
        begin = jnp.zeros((rows, keys), jnp.int32)
        for e in range(EPISODES):
            begin = jnp.where(start(e) <= pos, jnp.maximum(begin, start(e)), begin)
        for b in some:
            key_pos = info[BASES + at + b] + lax.broadcasted_iota(jnp.int32, (rows, keys), 1)
            allowed = (key_pos >= begin) & (key_pos <= pos)
            mask_ref[b] = jnp.where(allowed, 0.0, -1e30)

        def one(h):
            q = q_ref[:, h * HEAD : (h + 1) * HEAD]
            scores = [
                lax.dot_general(
                    q, ks[b][...], (((1,), (1,)), ((), ())), preferred_element_type=jnp.float32
                )
                + mask_ref[b]
                for b in some
            ]
            top = scores[0]
            for s in scores[1:]:
                top = jnp.maximum(top, s)
            top = jnp.max(top, axis=1, keepdims=True)
            if stage == "first":
                new = jnp.broadcast_to(top, (rows, HEAD))
                a = None
            else:
                old = m_in[head + h]
                new = jnp.maximum(old, top)
                shrink = jnp.exp2((old - new) * factor)
                a = a_in[head + h] * jnp.concatenate([shrink, shrink], axis=1)
            wide = jnp.concatenate([new] * (keys // HEAD), axis=1)
            for s, b in zip(scores, some):
                w = jnp.exp2((s - wide) * factor).astype(jnp.bfloat16)
                v = jnp.concatenate([vs[b][...], jnp.ones((keys, HEAD), jnp.bfloat16)], axis=1)
                product = jnp.dot(w, v, preferred_element_type=jnp.float32)
                a = product if a is None else a + product
            if final:
                divided(h, a)
            else:
                a_ref[head + h] = a
                m_ref[head + h] = new

        for h in range(per_group):
            one(h)

    if stage == "first":
        work([0])
    else:
        lives = []
        for b in range(count):
            base = info[BASES + at + b]
            lives.append((base < first) & (base + keys > lowest))
        several = list(range(min(count, 3)))
        if count > 1:
            every = lives[0] & lives[1] & lives[2]
            pair = lives[0] & lives[1] & jnp.logical_not(lives[2])
            pl.when(every)(functools.partial(work, several, False))
            pl.when(pair)(functools.partial(work, several[:2], False))
            for b in several:
                alone = lives[b] & jnp.logical_not(every | pair)
                pl.when(alone)(functools.partial(work, [b], False))
        if stage != "middle":
            pl.when(lives[-1])(functools.partial(work, [count - 1]))

            @pl.when(jnp.logical_not(lives[-1]))
            def _():
                for h in range(per_group):
                    divided(h, a_in[head + h])

    if stage == "own":
        for c in out_copies:
            c.start()
        for c in out_copies + came_copies:
            c.wait()


def attend(stage, scalars, at, queries, blocks, state=(), row=None, part=None, steps=4, extra=()):
    rows, width = queries[0].shape
    keys, columns = rows, blocks[0].shape[1]
    count = len(blocks)
    group = width // 2
    heads = ROWS_HERE * width // HEAD
    mask = pltpu.VMEM((count, rows, keys), jnp.float32)
    q_block = pltpu.VMEM((rows, group), jnp.bfloat16)
    if row is None:
        grid = (steps,)
        place = lambda g: (1 - g // 2, g % 2)
    elif part is not None:
        grid = (1,)
        place = lambda g: (row, part)
    else:
        grid = (2,)
        place = lambda g: (row, g)
    q_specs = [pl.BlockSpec((rows, group), lambda g: (0, place(g)[1]))] * len(queries)
    k_specs, v_specs = [], []
    for block in blocks:
        tall = block.shape[0] > keys
        at_k = lambda g, tall=tall: (place(g)[0] if tall else 0, place(g)[1])
        at_v = lambda g, f=at_k: (f(g)[0], columns // (2 * HEAD) + f(g)[1])
        k_specs.append(pl.BlockSpec((keys, HEAD), at_k))
        v_specs.append(pl.BlockSpec((keys, HEAD), at_v))
    in_specs = [SCALARS] + q_specs + k_specs + v_specs + [WHOLE] * len(state)
    aliases = {}
    if stage == "first" or stage == "middle":
        out_shape = [
            pltpu.VMEM((heads, rows, HEAD), jnp.float32),
            pltpu.VMEM((heads, rows, 2 * HEAD), jnp.float32),
        ]
        out_specs = [WHOLE, WHOLE]
        scratch = [mask]
        if row is None:
            scratch.append(q_block)
        if stage == "first":
            out_shape.append(pltpu.VMEM((rows, width), jnp.bfloat16))
            out_specs.append(WHOLE)
            scratch.append(pltpu.SemaphoreType.DMA((1, PIECES)))
            in_specs.append(ANYWHERE)
            extra = [pltpu.with_memory_space_constraint(v, pltpu.HBM) for v in extra]
        else:
            aliases = {len(in_specs) - 2: 0, len(in_specs) - 1: 1}
    elif stage == "other":
        out_shape, out_specs, scratch = pltpu.VMEM((rows, width), jnp.bfloat16), WHOLE, [mask]
    else:
        out_shape = [jax.ShapeDtypeStruct((rows, 2 * width), jnp.bfloat16)]
        out_specs = [ANYWHERE]
        if count > 1:
            aliases = {len(in_specs) - 2: 1, len(in_specs) - 1: 2}
            out_shape += [
                pltpu.VMEM((heads, rows, HEAD), jnp.float32),
                pltpu.VMEM((heads, rows, 2 * HEAD), jnp.float32),
            ]
            out_specs += [WHOLE, WHOLE]
        else:
            in_specs += [WHOLE, ANYWHERE]
            aliases = {len(in_specs) - 1: 0}
            extra = [pltpu.with_memory_space_constraint(extra[0], pltpu.VMEM), extra[1]]
        scratch = [mask, q_block, pltpu.SemaphoreType.DMA((2, PIECES))]
    state = [pltpu.with_memory_space_constraint(v, pltpu.VMEM) for v in state]
    return pl.pallas_call(
        functools.partial(
            attend_kernel,
            count=count,
            per_group=group // HEAD,
            stage=stage,
            at=at,
            row=row,
            part=part,
        ),
        grid=grid,
        in_specs=in_specs,
        out_specs=out_specs,
        out_shape=out_shape,
        input_output_aliases=aliases,
        scratch_shapes=scratch,
        compiler_params=params(14),
        cost_estimate=SHORT,
        name="attend_" + stage,
    )(in_smem(scalars), *queries, *blocks, *blocks, *state, *extra)


def body(
    hidden, queries, conv_input, norm_gain, kv_weight, conv_weight, conv_bias, starts, segment_ids
):
    del segment_ids
    rows = hidden.shape[1]
    ctx = lax.axis_index("ctx")
    me = ctx * FSDP + lax.axis_index("fsdp")
    x, zl = ctx // 2, ctx % 2
    depth = kv_weight.shape[0]
    leads = lax.axis_index("fsdp") % 2 == lead_core(x, zl)
    table = jnp.asarray(SLOTS)
    slots = jnp.stack([table[me], table[me ^ 1]])

    def base(dx, dz):
        return (((x + dx) % 4) * 2 + (zl + dz) % 2) * rows

    bases = [base(0, 0), base(0, 1), base(-1, 0), base(1, 0), base(-1, 1), base(2, 0), base(1, 1), base(2, 1)]
    core = lax.axis_index("fsdp") % 2
    flags = jnp.stack([leads.astype(jnp.int32), core])
    scalars = jnp.concatenate(
        [(ctx * rows)[None], starts[0], send(starts, SWAP)[0], jnp.stack(bases), flags]
    )
    signal = conv_input[0]
    tail = signal[rows - 16 :]
    flag = jnp.full((8, kv_weight.shape[1]), leads.astype(jnp.int32))
    slots, tail, scalars, flag = together(slots, tail, scalars, flag)

    w0 = kv_weight
    w1 = send(w0, WEIGHT_PAIRS[0])
    w2 = send(w0, WEIGHT_PAIRS[1])
    halo = lax.ppermute(tail, "ctx", [(i, i + 1) for i in range(CTX - 1)])
    mine, other = norm(slots, hidden[0], norm_gain[None], depth)
    w1, w2, halo, mine, other, scalars, flag = together(w1, w2, halo, mine, other, scalars, flag)

    w4 = send(w1, WEIGHT_PAIRS[3])
    theirs = send(other, SWAP)
    w5 = send(pick(flag, w1, w2), WEIGHT_PAIRS[4])
    theirs, scalars_later, w1_later = together(theirs, scalars, w1)
    w3 = send(w1_later, WEIGHT_PAIRS[2])
    q_theirs = send(split(scalars_later, queries[0]), SWAP)
    sums = project((mine, theirs), (0, 1), (w0, w1))

    w4, w5, q_theirs, *sums = together(w4, w5, q_theirs, *sums)
    w6 = send(w4, WEIGHT_PAIRS[5])
    w7 = send(pick(flag, w5, w4), WEIGHT_PAIRS[6])
    w8 = send(w5, WEIGHT_PAIRS[7])
    conv_out, token = conv(scalars, signal, halo, conv_weight, conv_bias[None])
    sums = project((mine, theirs), (2, 3, 4), (w3, w4, w5), sums, (token,))

    sums = project((mine, theirs), (6,), (w7,), sums)
    sums = project((mine, theirs), (5,), (w6,), sums)
    last = ((7,), ((w8, w2),))
    their_sum = finish(scalars, (theirs, mine), sums[::-1], *last, False)
    back = send(their_sum, SWAP)
    my_sum = finish(scalars, (mine, theirs), sums, *last, True)
    kv = add(my_sum, back)

    right_end = (0, 3)
    from_right = send(kv, moved("x-", lambda x, z: x in right_end))
    from_pair = send(kv, moved("zlo", lambda x, z: x < 3 or z == 1))
    from_left = send(kv, moved("x+", lambda x, z: x > 0))
    *state, q_mine = attend("first", scalars, 0, (q_theirs,), [kv], extra=(queries[0],))
    q = (q_mine, q_theirs)
    from_right, from_pair, *state = together(from_right, from_pair, *state)
    left_pair = send(from_pair, moved("x+", lambda x, z: x > 0))
    right_pair = send(from_right, moved("zlo", lambda x, z: x in right_end))
    far = send(from_right, moved("x-", lambda x, z: x > 1))
    state = attend("middle", scalars, 1, q, [from_pair, from_left, from_right], state)
    left_pair, right_pair, *state = together(left_pair, right_pair, *state)
    far_own = send(left_pair[:rows], moved("x+", lambda x, z: x > 1))
    far_other = send(right_pair[rows:], moved("x-", lambda x, z: x > 1))
    came = [left_pair, far, right_pair]
    state = attend("middle", scalars, 4, q, came, state, steps=3)
    far_own, far_other, *state = together(far_own, far_other, *state)
    for_other = attend("other", scalars, 7, (q_theirs,), [far_other], state, row=1)
    from_other = send(for_other, SWAP)
    attended, *state = attend(
        "own", scalars, 4, (q_mine,), [*came, far_own], state, row=0, part=1
    )
    (attended,) = attend(
        "own", scalars, 7, (q_mine,), [far_own], state, row=0, part=0, extra=(from_other, attended)
    )
    return attended[None], conv_out[None]


def solution(mesh):
    return jax.shard_map(
        body,
        mesh=mesh,
        in_specs=(
            P("fsdp", "ctx", None),
            P("fsdp", "ctx", None),
            P("fsdp", "ctx", None),
            P(),
            P("fsdp", None),
            P(),
            P(),
            P("fsdp", None),
            P("fsdp", "ctx"),
        ),
        out_specs=(P("fsdp", "ctx", None), P("fsdp", "ctx", None)),
        check_vma=False,
    )
```

```python
import functools
import math

import jax
import jax.numpy as jnp
import numpy as np
from jax import lax
from jax.experimental import pallas as pl
from jax.experimental.pallas import tpu as pltpu
from jax.sharding import PartitionSpec as P

HEAD = 128
TAPS = 4
EPISODES = 8
AXES = ("ctx", "fsdp")
CTX, FSDP = 8, 16
DEVICES = CTX * FSDP
MIB = 1 << 20


def place(i):
    c, f = divmod(i, FSDP)
    x, zl = divmod(c, 2)
    y, r = divmod(f, 4)
    zh, k = divmod(r, 2)
    return x, y, zh, zl, k


def device(x, y, zh, zl, k):
    return ((x % 4) * 2 + zl) * FSDP + ((y % 4) * 2 + zh) * 2 + k


def lead_core(x, zl):
    return (x + zl) % 2


def neighbour(x, y, zh, zl, way):
    return {
        "x+": (x + 1, y, zh, zl),
        "x-": (x - 1, y, zh, zl),
        "y+": (x, y + 1, zh, zl),
        "y-": (x, y - 1, zh, zl),
        "zlo": (x, y, zh, 1 - zl),
        "zhi": (x, y, 1 - zh, 1 - zl),
    }[way]


STEPS = (
    ((0, "y-", 0), (1, "zhi", 1)),
    ((0, "y+", 1),),
    ((0, "x-", 1), (1, "zlo", 0)),
    ((0, "y-", 0), (1, "y+", 1)),
    ((0, "zhi", 0), (1, "x+", 1)),
    ((0, "x-", 0), (1, "x+", 1)),
    ((0, "y-", 1), (1, "y+", 0)),
    ((0, "zlo", 0),),
)
SENT = ((0, 0), (0, 0), (1, 1), (1, 1), (1, 2), (4, 4), (5, 4), (5, 5))
SLOT_STEPS = ((0, 0), (1, 1), (3, 3), (4, 4), (5, 5), (6, 6), (7, 7), (8, 2))


def role_of(i):
    x, _, _, zl, k = place(i)
    return 0 if k == lead_core(x, zl) else 1


def weight_plan():
    pairs, held = [], [[i % FSDP for i in range(DEVICES)]]
    for step, sent in zip(STEPS, SENT):
        now, got = [], [-1] * DEVICES
        for i in range(DEVICES):
            for sender, way, receiver in step:
                if sender == role_of(i):
                    nx, ny, nzh, nzl = neighbour(*place(i)[:4], way)
                    lead = lead_core(nx, nzl)
                    to = device(nx, ny, nzh, nzl, lead if receiver == 0 else 1 - lead)
                    now.append((i, to))
                    got[to] = held[sent[role_of(i)]][i]
        pairs.append(now)
        held.append(got)
    slots = [[held[step[role_of(i)]][i] for step in SLOT_STEPS] for i in range(DEVICES)]
    return pairs, np.asarray(slots, np.int32)


WEIGHT_PAIRS, SLOTS = weight_plan()


def moved(way, wanted):
    pairs = [(i, device(*neighbour(*place(i)[:4], way), place(i)[4])) for i in range(DEVICES)]
    return [(i, to) for i, to in pairs if wanted(place(to)[0], place(to)[3])]


SWAP = [(i, i ^ 1) for i in range(DEVICES)]


def send(x, pairs):
    return lax.ppermute(x, AXES, pairs)


def together(*values):
    return lax.optimization_barrier(values)


def params(mib, **kw):
    return pltpu.CompilerParams(vmem_limit_bytes=mib * MIB, **kw)


WHOLE = pl.BlockSpec(memory_space=pltpu.VMEM)
SCALARS = pl.BlockSpec(memory_space=pltpu.SMEM)
ANYWHERE = pl.BlockSpec(memory_space=pl.ANY)
ROWS_HERE = 2
BLOCKS = 8
BASES = 1 + ROWS_HERE * EPISODES
LEAD = BASES + BLOCKS
CORE = LEAD + 1


def in_smem(scalars):
    return pltpu.with_memory_space_constraint(scalars, pltpu.SMEM)


SHORT = pl.CostEstimate(flops=1024, bytes_accessed=1024, transcendentals=0)


def norm_kernel(slots, h_ref, g_ref, mine_ref, other_ref, *, width, chunk, count):
    rows = h_ref.shape[0]
    here = pl.ds(pl.multiple_of(pl.program_id(0) * rows, rows), rows)
    total = jnp.zeros((rows, chunk), jnp.float32)
    for c in range(width // chunk):
        f = h_ref[:, c * chunk : (c + 1) * chunk].astype(jnp.float32)
        total = total + f * f
    mean = jnp.sum(total, axis=-1, keepdims=True) * (1.0 / width)
    factor = lax.rsqrt(mean + 1e-06)
    for which, out in ((1, other_ref), (0, mine_ref)):
        for s in range(count):
            at = pl.multiple_of(slots[which, s] * chunk, chunk)
            f = h_ref[:, pl.ds(at, chunk)].astype(jnp.float32)
            out[s, here, :] = (f * factor * g_ref[:, pl.ds(at, chunk)]).astype(jnp.bfloat16)


def norm(slots, hidden, gain, chunk):
    rows, width = hidden.shape
    count = slots.shape[1]
    tile = 64
    shape = pltpu.VMEM((count, rows, chunk), jnp.bfloat16)
    return pl.pallas_call(
        functools.partial(norm_kernel, width=width, chunk=chunk, count=count),
        grid=(rows // tile,),
        in_specs=[
            pl.BlockSpec(memory_space=pltpu.SMEM),
            pl.BlockSpec((tile, width), lambda i: (i, 0)),
            pl.BlockSpec((1, width), lambda i: (0, 0)),
        ],
        out_specs=[WHOLE, WHOLE],
        out_shape=[shape, shape],
        compiler_params=params(16),
        cost_estimate=SHORT,
        name="norm",
    )(slots, pltpu.with_memory_space_constraint(hidden, pltpu.HBM), gain)


def project_kernel(*refs, sides, slots, carried, after):
    del after
    count = len(slots)
    xs, ws = refs[:sides], refs[sides : sides + count]
    olds, outs = refs[sides + count :][:carried], refs[-sides:]
    tile = 256
    for s in range(count):
        for c in range(0, ws[s].shape[1], tile):
            cols = slice(c, c + tile)
            w = ws[s][:, cols]
            for side in range(sides):
                part = jnp.dot(xs[side][slots[s]], w, preferred_element_type=jnp.float32)
                if s:
                    part = outs[side][:, cols] + part
                elif carried:
                    part = olds[side][:, cols] + part
                outs[side][:, cols] = part


def project(xs, slots, weights, carried=(), after=()):
    _, rows, depth = xs[0].shape
    columns = weights[0].shape[1]
    sides = len(xs)
    inside = [
        pltpu.with_memory_space_constraint(v, pltpu.VMEM) for v in (*xs, *weights, *carried, *after)
    ]
    return pl.pallas_call(
        functools.partial(
            project_kernel, sides=sides, slots=slots, carried=len(carried), after=len(after)
        ),
        in_specs=[WHOLE] * len(inside),
        out_specs=[WHOLE] * sides,
        out_shape=[pltpu.VMEM((rows, columns), jnp.float32)] * sides,
        compiler_params=params(8),
        cost_estimate=SHORT,
        name="project",
    )(*inside)


def pick_kernel(flag_ref, a_ref, b_ref, o_ref):
    o_ref[...] = jnp.where(flag_ref[0:1, :] > 0, a_ref[...], b_ref[...])


def pick(flag, a, b):
    inside = [pltpu.with_memory_space_constraint(v, pltpu.VMEM) for v in (flag, a, b)]
    return pl.pallas_call(
        pick_kernel,
        in_specs=[WHOLE] * 3,
        out_specs=WHOLE,
        out_shape=pltpu.VMEM(a.shape, a.dtype),
        compiler_params=params(8),
        cost_estimate=SHORT,
        name="pick",
    )(*inside)


def finish_kernel(scalars, x0, x1, old0, old1, *refs, slots, counts, own):
    ws, out = refs[:-1], refs[-1]
    rows, tile = old0.shape[0], out.shape[1] // 2
    core = scalars[CORE] if own else 1 - scalars[CORE]
    for part in range(2):
        cols = pl.ds(pl.multiple_of((2 * part + core) * tile, tile), tile)
        for side, (x, old) in enumerate(((x0, old0), (x1, old1))):
            total = old[:, cols]
            at = 0
            for s, n in enumerate(counts):
                w = ws[at][:, cols]
                if n == 2:
                    w = jnp.where(scalars[LEAD] > 0, w, ws[at + 1][:, cols])
                total = total + jnp.dot(x[slots[s]], w, preferred_element_type=jnp.float32)
                at += n
            out[side * rows : (side + 1) * rows, part * tile : (part + 1) * tile] = total


def finish(scalars, xs, olds, slots, weights, own):
    weights = [w if isinstance(w, tuple) else (w,) for w in weights]
    counts = tuple(len(w) for w in weights)
    flat = [v for w in weights for v in w]
    rows, columns = olds[0].shape
    inside = [pltpu.with_memory_space_constraint(v, pltpu.VMEM) for v in (*xs, *olds, *flat)]
    depth = xs[0].shape[2]
    return pl.pallas_call(
        functools.partial(finish_kernel, slots=slots, counts=counts, own=own),
        in_specs=[SCALARS] + [WHOLE] * len(inside),
        out_specs=WHOLE,
        out_shape=pltpu.VMEM((2 * rows, columns // 2), jnp.float32),
        compiler_params=params(8),
        cost_estimate=SHORT,
        name="finish",
    )(in_smem(scalars), *inside)


def add_kernel(a_ref, b_ref, o_ref):
    o_ref[...] = (a_ref[...] + b_ref[...]).astype(o_ref.dtype)


def add(a, b):
    inside = [pltpu.with_memory_space_constraint(v, pltpu.VMEM) for v in (a, b)]
    return pl.pallas_call(
        add_kernel,
        in_specs=[WHOLE, WHOLE],
        out_specs=WHOLE,
        out_shape=pltpu.VMEM(a.shape, jnp.bfloat16),
        compiler_params=params(8),
        cost_estimate=SHORT,
        name="add",
    )(*inside)


PIECES = 8


def copies_of(pairs, sems):
    copies = []
    for i, (source, target, rows) in enumerate(pairs):
        step = rows // PIECES
        for p in range(PIECES):
            here = pl.ds(p * step, step)
            copies.append(pltpu.make_async_copy(source(here), target(here), sems.at[i, p]))
    return copies


def split_kernel(scalars, q_ref, out_ref, sems):
    rows, width = out_ref.shape
    cols = pl.ds(pl.multiple_of((1 - scalars[CORE]) * width, width), width)
    copies = copies_of([(lambda r: q_ref.at[r, cols], lambda r: out_ref.at[r, :], rows)], sems)
    for c in copies:
        c.start()
    for c in copies:
        c.wait()


def split(scalars, queries):
    rows, width = queries.shape
    return pl.pallas_call(
        split_kernel,
        in_specs=[SCALARS, ANYWHERE],
        out_specs=WHOLE,
        out_shape=pltpu.VMEM((rows, width // 2), queries.dtype),
        scratch_shapes=[pltpu.SemaphoreType.DMA((1, PIECES))],
        compiler_params=params(8),
        cost_estimate=SHORT,
        name="split",
    )(in_smem(scalars), pltpu.with_memory_space_constraint(queries, pltpu.HBM))


def merge_kernel(scalars, part_ref, all_in, all_ref, sems):
    del all_in
    rows, width = part_ref.shape
    cols = pl.ds(pl.multiple_of((1 - scalars[CORE]) * width, width), width)
    copies = copies_of(
        [(lambda r: part_ref.at[r, :], lambda r: all_ref.at[r, cols], rows)], sems
    )
    for c in copies:
        c.start()
    for c in copies:
        c.wait()


def merge(scalars, part, whole):
    return pl.pallas_call(
        merge_kernel,
        in_specs=[SCALARS, WHOLE, ANYWHERE],
        out_specs=ANYWHERE,
        out_shape=jax.ShapeDtypeStruct(whole.shape, whole.dtype),
        input_output_aliases={2: 0},
        scratch_shapes=[pltpu.SemaphoreType.DMA((1, PIECES))],
        compiler_params=params(8),
        cost_estimate=SHORT,
        name="merge",
    )(in_smem(scalars), pltpu.with_memory_space_constraint(part, pltpu.VMEM), whole)


def conv_kernel(info, x_ref, halo_ref, w_ref, b_ref, o_ref, token, pick, before):
    rows, width = x_ref.shape
    ahead = halo_ref.shape[0]
    token[...] = jnp.zeros_like(token)

    @pl.when(pl.program_id(0) == 0)
    def _():
        before[...] = halo_ref[...]

    shape = (rows, ahead + rows)
    pos = info[0] + pl.program_id(0) * rows + lax.broadcasted_iota(jnp.int32, shape, 0)
    begin = jnp.zeros(shape, jnp.int32)
    for e in range(EPISODES):
        begin = jnp.where(info[1 + e] <= pos, jnp.maximum(begin, info[1 + e]), begin)
    apart = lax.broadcasted_iota(jnp.int32, shape, 0) + ahead - lax.broadcasted_iota(jnp.int32, shape, 1)
    for tap in range(TAPS):
        behind = TAPS - 1 - tap
        taken = (apart == behind) & (pos - behind >= begin)
        pick[tap * rows : (tap + 1) * rows, :] = jnp.where(taken, 1.0, 0.0).astype(pick.dtype)

    lanes = 256
    for c in range(0, width, lanes):
        cols = slice(c, c + lanes)
        source = jnp.concatenate([before[:, cols], x_ref[:, cols]], axis=0)
        taps = jnp.dot(pick[...], source, preferred_element_type=jnp.float32)
        mixing = b_ref[:, cols] + taps[:rows] * w_ref[0:1, cols]
        for tap in range(1, TAPS):
            mixing = mixing + taps[tap * rows : (tap + 1) * rows] * w_ref[tap : tap + 1, cols]
        by_half = 0.5 * mixing
        o_ref[:, cols] = (by_half + by_half * jnp.tanh(by_half)).astype(o_ref.dtype)
    before[...] = x_ref[rows - ahead :, :]


def conv(info, x, halo, weight, bias):
    rows, width = x.shape
    tile = 64
    ahead = halo.shape[0]
    full = lambda n: pl.BlockSpec((n, width), lambda i: (0, 0))
    return pl.pallas_call(
        conv_kernel,
        grid=(rows // tile,),
        in_specs=[
            SCALARS,
            pl.BlockSpec((tile, width), lambda i: (i, 0)),
            full(ahead),
            full(TAPS),
            full(1),
        ],
        out_specs=[pl.BlockSpec((tile, width), lambda i: (i, 0)), WHOLE],
        out_shape=[
            jax.ShapeDtypeStruct((rows, width), x.dtype),
            pltpu.VMEM((8, 128), jnp.float32),
        ],
        scratch_shapes=[
            pltpu.VMEM((TAPS * tile, ahead + tile), jnp.bfloat16),
            pltpu.VMEM((ahead, width), x.dtype),
        ],
        compiler_params=params(16),
        cost_estimate=SHORT,
        name="conv",
    )(in_smem(info), x, halo, weight, bias)


def attend_kernel(info, *refs, count, per_group, stage, at, row):
    if stage == "first":
        q1_ref, *refs = refs
    else:
        q0_ref, q1_ref, *refs = refs
    ks, vs = refs[:count], refs[count : 2 * count]
    rest = refs[2 * count :]
    if stage == "first":
        q_hbm, m_ref, a_ref, own_ref, q_ref, mask_ref, q_sems = rest
        m_in, a_in = m_ref, a_ref
    elif stage == "middle":
        m_in, a_in, m_ref, a_ref, q_ref, mask_ref = rest
    elif row:
        m_in, a_in, o_ref, q_ref, mask_ref = rest
    else:
        m_in, a_in, o_hbm, q_ref, mask_ref, o_buf, sems = rest
    rows, keys = mask_ref.shape[1:]
    factor = math.log2(math.e) / math.sqrt(HEAD)
    first = info[0]
    if stage == "last":
        here, group = row, pl.program_id(0)
        q_ref = q1_ref if row else q0_ref
    else:
        here, group = 1 - pl.program_id(0) // 2, pl.program_id(0) % 2
    if stage == "middle":
        q_ref[...] = jnp.where(here == 0, q0_ref[...], q1_ref[...])
    if stage == "first":
        width = own_ref.shape[1]
        cols = pl.ds(pl.multiple_of(info[CORE] * width, width), width)
        copies = copies_of(
            [(lambda r: q_hbm.at[r, cols], lambda r: own_ref.at[r, :], own_ref.shape[0])], q_sems
        )

        @pl.when(pl.program_id(0) == 0)
        def _():
            for c in copies:
                c.start()

        @pl.when(pl.program_id(0) == 2)
        def _():
            for c in copies:
                c.wait()

        @pl.when(here == 0)
        def _():
            part = q_ref.shape[1]
            q_ref[...] = own_ref[:, pl.ds(pl.multiple_of(group * part, part), part)]

        @pl.when(here == 1)
        def _():
            q_ref[...] = q1_ref[...]

    if stage == "last" and not row:
        o_ref = o_buf.at[group]

    def start(e):
        return info[1 + here * EPISODES + e]

    lowest = jnp.int32(0)
    for e in range(EPISODES):
        lowest = jnp.where(start(e) <= first, jnp.maximum(lowest, start(e)), lowest)
    head = (here * 2 + group) * per_group

    def divided(h, a):
        value = (a[:, :HEAD] / a[:, HEAD:]).astype(jnp.bfloat16)
        if row:
            part = per_group * HEAD
            at_column = pl.multiple_of(group * part, part) + h * HEAD
            o_ref[:, pl.ds(pl.multiple_of(at_column, HEAD), HEAD)] = value
        else:
            o_ref[:, h * HEAD : (h + 1) * HEAD] = value

    def work(some):
        pos = first + lax.broadcasted_iota(jnp.int32, (rows, keys), 0)
        begin = jnp.zeros((rows, keys), jnp.int32)
        for e in range(EPISODES):
            begin = jnp.where(start(e) <= pos, jnp.maximum(begin, start(e)), begin)
        for b in some:
            key_pos = info[BASES + at + b] + lax.broadcasted_iota(jnp.int32, (rows, keys), 1)
            allowed = (key_pos >= begin) & (key_pos <= pos)
            mask_ref[b] = jnp.where(allowed, 0.0, -1e30)
        k = [ks[b][...] for b in some]
        v = [jnp.concatenate([vs[b][...], jnp.ones((keys, HEAD), jnp.bfloat16)], axis=1) for b in some]
        for h in range(per_group):
            q = q_ref[:, h * HEAD : (h + 1) * HEAD]
            scores = [
                lax.dot_general(q, k_b, (((1,), (1,)), ((), ())), preferred_element_type=jnp.float32)
                + mask_ref[b]
                for b, k_b in zip(some, k)
            ]
            top = scores[0]
            for s in scores[1:]:
                top = jnp.maximum(top, s)
            top = jnp.max(top, axis=1, keepdims=True)
            if stage == "first":
                new = jnp.broadcast_to(top, (rows, HEAD))
                a = None
            else:
                old = m_in[head + h]
                new = jnp.maximum(old, top)
                shrink = jnp.exp2((old - new) * factor)
                a = a_in[head + h] * jnp.concatenate([shrink, shrink], axis=1)
            wide = jnp.concatenate([new] * (keys // HEAD), axis=1)
            for s, v_b in zip(scores, v):
                w = jnp.exp2((s - wide) * factor).astype(jnp.bfloat16)
                part = jnp.dot(w, v_b, preferred_element_type=jnp.float32)
                a = part if a is None else a + part
            if stage == "last":
                divided(h, a)
            else:
                a_ref[head + h] = a
                m_ref[head + h] = new

    if stage == "first":
        work([0])
    else:
        lives = []
        for b in range(count):
            base = info[BASES + at + b]
            lives.append((base < first) & (base + keys > lowest))
        done = functools.reduce(jnp.logical_and, lives)
        pl.when(done)(functools.partial(work, list(range(count))))
        if count > 2:
            pair = lives[0] & lives[1] & jnp.logical_not(done)
            pl.when(pair)(functools.partial(work, [0, 1]))
            done = done | pair
        if count > 1:
            for b in range(count):
                pl.when(lives[b] & jnp.logical_not(done))(functools.partial(work, [b]))
        if stage == "last":

            @pl.when(jnp.logical_not(done))
            def _():
                for h in range(per_group):
                    divided(h, a_in[head + h])

    if stage == "last" and not row:
        width = o_buf.shape[2]

        def out_copy(j):
            cols = pl.ds(pl.multiple_of((info[CORE] * 2 + j) * width, width), width)
            return pltpu.make_async_copy(o_buf.at[j], o_hbm.at[:, cols], sems.at[j])

        out_copy(group).start()

        @pl.when(group == 1)
        def _():
            out_copy(0).wait()
            out_copy(1).wait()


def attend(stage, scalars, at, queries, blocks, state=(), row=None, whole=None):
    rows, width = queries[0].shape
    columns = blocks[0].shape[1]
    keys = blocks[0].shape[0] // (1 if stage == "last" else ROWS_HERE)
    count = len(blocks)
    group = width // 2
    heads = ROWS_HERE * width // HEAD
    scratch = [pltpu.VMEM((rows, group), jnp.bfloat16), pltpu.VMEM((count, rows, keys), jnp.float32)]
    half_columns = columns // (2 * HEAD)
    if stage == "last":
        grid = (2,)
        q_specs = [pl.BlockSpec((rows, group), lambda g: (0, g))] * 2
        k_spec = pl.BlockSpec((keys, HEAD), lambda g: (0, g))
        v_spec = pl.BlockSpec((keys, HEAD), lambda g: (0, half_columns + g))
        if row:
            out_shape = pltpu.VMEM((rows, width), jnp.bfloat16)
            out_specs = WHOLE
        else:
            out_shape = jax.ShapeDtypeStruct((rows, 2 * width), jnp.bfloat16)
            out_specs = ANYWHERE
            scratch += [pltpu.VMEM((2, rows, group), jnp.bfloat16), pltpu.SemaphoreType.DMA((2,))]
    else:
        grid = (4,)
        q_specs = [pl.BlockSpec((rows, group), lambda g: (0, g % 2))] * 2
        k_spec = pl.BlockSpec((keys, HEAD), lambda g: (1 - g // 2, g % 2))
        v_spec = pl.BlockSpec((keys, HEAD), lambda g: (1 - g // 2, half_columns + g % 2))
        out_shape = [
            pltpu.VMEM((heads, rows, HEAD), jnp.float32),
            pltpu.VMEM((heads, rows, 2 * HEAD), jnp.float32),
        ]
        out_specs = [WHOLE, WHOLE]
        if stage == "first":
            out_shape.append(pltpu.VMEM((rows, width), jnp.bfloat16))
            out_specs.append(WHOLE)
            scratch.append(pltpu.SemaphoreType.DMA((1, PIECES)))
            q_specs = q_specs[1:]
    in_specs = [SCALARS] + q_specs + [k_spec] * count + [v_spec] * count + [WHOLE] * len(state)
    extra = []
    if stage == "first":
        in_specs.append(ANYWHERE)
        extra = [pltpu.with_memory_space_constraint(whole, pltpu.HBM)]
    aliases = {} if stage != "middle" else {len(in_specs) - 2: 0, len(in_specs) - 1: 1}
    state = [pltpu.with_memory_space_constraint(v, pltpu.VMEM) for v in state]
    return pl.pallas_call(
        functools.partial(
            attend_kernel, count=count, per_group=group // HEAD, stage=stage, at=at, row=row
        ),
        grid=grid,
        in_specs=in_specs,
        out_specs=out_specs,
        out_shape=out_shape,
        input_output_aliases=aliases,
        scratch_shapes=scratch,
        compiler_params=params(14),
        cost_estimate=SHORT,
        name="attend_" + stage,
    )(in_smem(scalars), *queries, *blocks, *blocks, *state, *extra)


def body(
    hidden, queries, conv_input, norm_gain, kv_weight, conv_weight, conv_bias, starts, segment_ids
):
    del segment_ids
    rows = hidden.shape[1]
    ctx = lax.axis_index("ctx")
    me = ctx * FSDP + lax.axis_index("fsdp")
    x, zl = ctx // 2, ctx % 2
    depth = kv_weight.shape[0]
    leads = lax.axis_index("fsdp") % 2 == lead_core(x, zl)
    table = jnp.asarray(SLOTS)
    slots = jnp.stack([table[me], table[me ^ 1]])

    def base(dx, dz):
        return (((x + dx) % 4) * 2 + (zl + dz) % 2) * rows

    bases = [base(0, 0), base(0, 1), base(-1, 0), base(1, 0), base(-1, 1), base(2, 0), base(1, 1), base(2, 1)]
    core = lax.axis_index("fsdp") % 2
    flags = jnp.stack([leads.astype(jnp.int32), core])
    scalars = jnp.concatenate(
        [(ctx * rows)[None], starts[0], send(starts, SWAP)[0], jnp.stack(bases), flags]
    )
    signal = conv_input[0]
    tail = signal[rows - 16 :]
    flag = jnp.full((8, kv_weight.shape[1]), leads.astype(jnp.int32))
    slots, tail, scalars, flag = together(slots, tail, scalars, flag)

    w0 = kv_weight
    w1 = send(w0, WEIGHT_PAIRS[0])
    w2 = send(w0, WEIGHT_PAIRS[1])
    halo = lax.ppermute(tail, "ctx", [(i, i + 1) for i in range(CTX - 1)])
    mine, other = norm(slots, hidden[0], norm_gain[None], depth)
    w1, w2, halo, mine, other, scalars, flag = together(w1, w2, halo, mine, other, scalars, flag)

    w4 = send(w1, WEIGHT_PAIRS[3])
    theirs = send(other, SWAP)
    w5 = send(pick(flag, w1, w2), WEIGHT_PAIRS[4])
    theirs, scalars_later, w1_later = together(theirs, scalars, w1)
    w3 = send(w1_later, WEIGHT_PAIRS[2])
    q_theirs = send(split(scalars_later, queries[0]), SWAP)
    sums = project((mine, theirs), (0, 1), (w0, w1))

    w4, w5, q_theirs, *sums = together(w4, w5, q_theirs, *sums)
    w6 = send(w4, WEIGHT_PAIRS[5])
    w7 = send(pick(flag, w5, w4), WEIGHT_PAIRS[6])
    w8 = send(w5, WEIGHT_PAIRS[7])
    conv_out, token = conv(scalars, signal, halo, conv_weight, conv_bias[None])
    sums = project((mine, theirs), (2, 3, 4), (w3, w4, w5), sums, (token,))

    sums = project((mine, theirs), (6,), (w7,), sums)
    sums = project((mine, theirs), (5,), (w6,), sums)
    last = ((7,), ((w8, w2),))
    their_sum = finish(scalars, (theirs, mine), sums[::-1], *last, False)
    back = send(their_sum, SWAP)
    my_sum = finish(scalars, (mine, theirs), sums, *last, True)
    kv = add(my_sum, back)

    right_end = (0, 3)
    from_right = send(kv, moved("x-", lambda x, z: x in right_end))
    from_pair = send(kv, moved("zlo", lambda x, z: x < 3 or z == 1))
    from_left = send(kv, moved("x+", lambda x, z: x > 0))
    *state, q_mine = attend("first", scalars, 0, (q_theirs,), [kv], whole=queries[0])
    q = (q_mine, q_theirs)
    from_right, from_pair, *state = together(from_right, from_pair, *state)
    left_pair = send(from_pair, moved("x+", lambda x, z: x > 0))
    right_pair = send(from_right, moved("zlo", lambda x, z: x in right_end))
    far = send(from_right, moved("x-", lambda x, z: x > 1))
    state = attend("middle", scalars, 1, q, [from_pair, from_left, from_right], state)
    left_pair, right_pair, *state = together(left_pair, right_pair, *state)
    far_own = send(left_pair[:rows], moved("x+", lambda x, z: x > 1))
    far_other = send(right_pair[rows:], moved("x-", lambda x, z: x > 1))
    state = attend("middle", scalars, 4, q, [left_pair, far, right_pair], state)
    far_own, far_other, *state = together(far_own, far_other, *state)
    for_other = attend("last", scalars, 7, q, [far_other], state, row=1)
    from_other = send(for_other, SWAP)
    attended = attend("last", scalars, 7, q, [far_own], state, row=0)
    attended = merge(scalars, from_other, attended)
    return attended[None], conv_out[None]


def solution(mesh):
    return jax.shard_map(
        body,
        mesh=mesh,
        in_specs=(
            P("fsdp", "ctx", None),
            P("fsdp", "ctx", None),
            P("fsdp", "ctx", None),
            P(),
            P("fsdp", None),
            P(),
            P(),
            P("fsdp", None),
            P("fsdp", "ctx"),
        ),
        out_specs=(P("fsdp", "ctx", None), P("fsdp", "ctx", None)),
        check_vma=False,
    )
```
